256 devices in a mesh: rep: 4 (over z_hi, core), fsdp: 64 (over y, x, z_lo).
Axes of the slice: x: 4, y: 4, z: 8 (z_hi: 2, z_lo: 4; z = z_hi * 4 + z_lo), core: 2. Of those that a mesh axis runs over, the one named last changes fastest.
Arguments:
- features: bfloat16 [14336, 4096], P(('rep', 'fsdp')), may hold values from -6 to 6
- cotangent: bfloat16 [14336, 14336], P('rep', 'fsdp'), may hold values from -6 to 6
- up_rows: bfloat16 [14336, 4096], P('fsdp'), may hold values from -0.09375 to 0.09375
- moment: float32 [14336, 4096], P('fsdp'), may hold values from -4 to 4
- exponents: int32 [14336, 32], P('fsdp'), may hold values from -11 to -8
Outputs:
- new_params: bfloat16 [14336, 4096], P('fsdp')
- new_moment: float32 [14336, 4096], P('fsdp')
The draws below stay inside these ranges and needn't reach their ends.
All inputs are finite; a program needn't handle non-finite values.
Results may differ from the reference program's by a relative error of at most 0.013.
Values may be sent and summed in bfloat16 or wider, within the bound.
A program may use at most 128 MiB of HBM per device.

```python
import jax
import jax.numpy as jnp
from jax import lax

D = 4096
FF = 14336
GROUP_TOK = 3584
TOKENS = 14336
N_REP = 4


def touch_ends(result, rng, smallest, largest):
    longest = result.shape.index(max(result.shape))
    spots = []
    for shift in (0, 1):
        where = [jax.random.randint(jax.random.fold_in(rng, axis), (), 0, length) for axis, length in enumerate(result.shape)]
        where[longest] = (where[longest] + shift) % result.shape[longest]
        spots.append(tuple(where))
    return result.at[spots[0]].set(smallest).at[spots[1]].set(largest)


def level_of(stream_key, extent, shards, least, largest):
    gain, own = 1.0, jax.random.fold_in(stream_key, 6)
    for axis_at, shards_of in shards:
        heights = jnp.exp(jax.random.uniform(jax.random.fold_in(own, axis_at), (shards_of,), jnp.float32, least / len(shards), largest / len(shards)))
        gain = gain * jnp.repeat(heights, extent[axis_at] // shards_of).reshape([-1 if axis == axis_at else 1 for axis in range(len(extent))])
    return gain


def scatter_about(stream_key, extent, deviation, reach, cuts=(), kind=jnp.bfloat16):
    result = jax.random.normal(stream_key, extent, jnp.float32) * deviation
    if len(cuts) > 0:
        result = level_of(stream_key, extent, cuts, -0.22, 0.18) * result
    return jnp.clip(result, min=-reach, max=reach).astype(kind)


def setup_inputs(seed: int = 0) -> dict:
    streams_of = jax.random.split(jax.random.key(seed), 6)
    return {
        "features": scatter_about(streams_of[0], (TOKENS, D), 1.0, 6.0, ((0, 256),)),
        "cotangent": scatter_about(streams_of[1], (TOKENS, FF), 1.0, 6.0, ((0, 4), (1, 64))),
        "up_rows": scatter_about(streams_of[2], (FF, D), D ** -0.5, 0.09375, ((0, 64),)),
        "moment": scatter_about(streams_of[3], (FF, D), 0.3, 4.0, ((0, 64),), jnp.float32),
        "exponents": touch_ends(jax.random.randint(streams_of[4], (FF, D // 128), -11, -7), jax.random.fold_in(streams_of[4], 1), -11, (-7) - 1).astype(jnp.int32),
    }


inner_rate = 0.02
outer_rate = 0.7
momentum_coef = 0.9
code_limit = 448.0


def silu_slope(preact):
    squashed = jax.nn.sigmoid(preact)
    return squashed * (1.0 + preact * (1.0 - squashed))


def encode_blocks(gradient, scales):
    shard_rows, model_width = gradient.shape
    blocked = gradient.reshape(shard_rows, model_width // 128, 128) * jnp.exp2(-scales)[:, :, None]
    clipped = jnp.clip(inner_rate * blocked, -code_limit, code_limit).astype(jnp.bfloat16)
    return lax.optimization_barrier(clipped).astype(jnp.float32).reshape(shard_rows, model_width)


def nesterov_step(summed, scales, params, moment, groups):
    shard_rows, model_width = summed.shape
    blocked = summed.reshape(shard_rows, model_width // 128, 128) * jnp.exp2(scales)[:, :, None]
    decoded = blocked.reshape(shard_rows, model_width) / groups
    new_moment = momentum_coef * moment + decoded
    new_params = (params.astype(jnp.float32) - outer_rate * (decoded + momentum_coef * new_moment)).astype(jnp.bfloat16)
    return new_params, new_moment


def reference(features, cotangent, up_rows, moment, exponents):
    scales = exponents.astype(jnp.float32)
    inputs_all = features.reshape(N_REP, GROUP_TOK, D)
    upstream_all = cotangent.reshape(N_REP, GROUP_TOK, FF)
    summed = jnp.zeros((FF, D), jnp.float32)
    for group in range(N_REP):
        inputs = inputs_all[group]
        upstream = upstream_all[group]
        preact = jnp.dot(inputs, up_rows.T, preferred_element_type=jnp.float32)
        hidden_grad = (upstream.astype(jnp.float32) * silu_slope(preact)).astype(jnp.bfloat16)
        gradient = jnp.dot(hidden_grad.T, inputs, preferred_element_type=jnp.float32)
        summed = summed + encode_blocks(gradient, scales)
    return nesterov_step(summed, scales, up_rows, moment, float(N_REP))
```

```python
import functools

import jax
import jax.numpy as jnp
from jax import lax
from jax.experimental import pallas as pl
from jax.experimental.pallas import tpu as pltpu
from jax.sharding import PartitionSpec as P

inner_rate = 0.02
outer_rate = 0.7
momentum_coef = 0.9
code_limit = 448.0

D = 4096
HALF = D // 2
TOK = 56
SEED = 2 * TOK
CLASS_TOK = 1792
ROWS = 224
HROWS = ROWS // 2
MESH = pl.DeviceIdType.MESH
ANY = pl.BlockSpec(memory_space=pl.ANY)


def where_am_i():
    rep, at = lax.axis_index("rep"), lax.axis_index("fsdp")
    return rep // 2, rep % 2, at // 16, (at // 4) % 4, at % 4


def device(zh, c, y, x, z):
    return (zh * 2 + c, (y * 4 + x) * 4 + z)


def barrier(peers):
    sem = pltpu.get_barrier_semaphore()
    for peer in peers:
        pl.semaphore_signal(sem, inc=1, device_id=peer, device_id_type=MESH)
    pl.semaphore_wait(sem, len(peers))


def remote(src, dst, send_sem, recv_sem, peer):
    return pltpu.make_async_remote_copy(src, dst, send_sem, recv_sem, device_id=peer, device_id_type=MESH)


def seed_kernel(f_ref, o_ref, send, recv, local):
    zh, c, y, x, z = where_am_i()
    mirror = 3 - x
    barrier([device(zh, 1 - c, y, x, z), device(zh, 0, y, mirror, z), device(zh, 1, y, mirror, z)])
    slot = x // 2

    def half(k):
        return f_ref.at[:, pl.ds(pl.multiple_of(k * HALF, HALF), HALF)]

    @pl.when(c == x // 2)
    def _():
        keep = pltpu.make_async_copy(half(c), o_ref.at[slot], local)
        give = remote(half(1 - c), o_ref.at[slot], send.at[0], recv.at[slot], device(zh, 1 - c, y, x, z))
        keep.start()
        give.start()
        keep.wait()
        give.wait_send()
        remote(half(0), o_ref.at[1 - slot], send.at[0], recv.at[1 - slot], device(zh, 1 - c, y, x, z)).wait_recv()

    @pl.when(c != x // 2)
    def _():
        sends = [remote(half(k), o_ref.at[slot], send.at[k], recv.at[slot], device(zh, k, y, mirror, z)) for k in range(2)]
        for s in sends:
            s.start()
        for s in sends:
            s.wait_send()
        for k in range(2):
            remote(half(0), o_ref.at[k], send.at[0], recv.at[k], device(zh, 1 - c, y, x, z)).wait_recv()


def gather_kernel(s_ref, w_ref, d_ref, x_ref, wg_ref, dg_ref, zsend, zrecv, ysend, yrecv, csend, crecv, wsend, wrecv, dsend, drecv, local):
    zh, c, y, x, z = where_am_i()

    def at_y(k):
        return device(zh, c, (y + k) % 4, x, z)

    sibling = device(zh, 1 - c, y, x, z)
    peers = [sibling, at_y(1), at_y(3)]
    peers += [device(zh, c, y, x, (z + k) % 4) for k in range(1, 4)]
    peers += [device(zh, k, y, (x + q) % 4, z) for q in range(1, 4) for k in range(2)]
    barrier(peers)

    def place(yy, zz, core, lo=0, n=SEED):
        row = pl.multiple_of((yy * 4 + zz) * SEED + lo, 16)
        return x_ref.at[pl.ds(row, n), pl.ds(pl.multiple_of(core * HALF, HALF), HALF)]

    keep = pltpu.make_async_copy(s_ref, place(y, z, c), local.at[0])
    keep.start()
    zs = [remote(s_ref, place(y, z, c), zsend.at[k], zrecv.at[k], device(zh, c, y, x, (z + k) % 4)) for k in range(1, 4)]
    for s in zs:
        s.start()
    ws = []
    for d in range(1, 4):
        rows = pl.ds(pl.multiple_of(c * HROWS, 16), HROWS)
        ws.append(remote(w_ref.at[rows], wg_ref.at[d % 2, rows], wsend.at[d], wrecv.at[d % 2, c], device(zh, d // 2, y, (x + 4 - d) % 4, z)))
    for s in ws:
        s.start()
    keep_w = pltpu.make_async_copy(w_ref, wg_ref.at[0], local.at[1])

    @pl.when(c == 0)
    def _():
        keep_w.start()

    keep_d = pltpu.make_async_copy(d_ref.at[0], dg_ref.at[0], local.at[2])
    for k in range(2):
        to = 2 * c + k
        d = (x - to + 4) % 4
        h = jnp.where((to == 0) | (to == 3), 0, 1)
        mine = (d == 0) & (c == 0)

        @pl.when(mine)
        def _():
            pltpu.make_async_copy(d_ref.at[h], dg_ref.at[0], local.at[2]).start()

        @pl.when(jnp.logical_not(mine))
        def _():
            remote(d_ref.at[h], dg_ref.at[d % 2], dsend.at[k], drecv.at[d % 2], device(zh, d // 2, y, to, z)).start()

    def arrived(k, zz):
        src = s_ref if k == 0 else place(y, zz, c)
        both = [remote(src, place(y, zz, c), ysend.at[k, 0], yrecv.at[k, 0], at_y(1)),
                remote(src, place(y, zz, c), ysend.at[k, 1], yrecv.at[k, 1], at_y(3)),
                remote(src, place(y, zz, c), csend.at[k, 0], crecv.at[k, 0], sibling)]
        for s in both:
            s.start()

    cut = 64
    arrived(0, z)
    for k in (1, 3, 2):
        remote(s_ref, place(y, z, c), zsend.at[k], zrecv.at[k], sibling).wait_recv()
        arrived(k, (z + 4 - k) % 4)
    for k in (0, 1, 3, 2):
        zz = (z + 4 - k) % 4
        up = remote(s_ref, place((y + 3) % 4, zz, c), ysend.at[k, 0], yrecv.at[k, 0], at_y(1))
        up.wait_recv()
        remote(place((y + 3) % 4, zz, c, 0, cut), place((y + 3) % 4, zz, c, 0, cut), ysend.at[k, 2], yrecv.at[k, 2], at_y(1)).start()
        remote(place((y + 3) % 4, zz, c), place((y + 3) % 4, zz, c), csend.at[k, 1], crecv.at[k, 1], sibling).start()
        down = remote(s_ref, place((y + 1) % 4, zz, c), ysend.at[k, 1], yrecv.at[k, 1], at_y(3))
        down.wait_recv()
        remote(place((y + 1) % 4, zz, c, cut, SEED - cut), place((y + 1) % 4, zz, c, cut, SEED - cut), ysend.at[k, 3], yrecv.at[k, 3], at_y(3)).start()
        remote(place((y + 1) % 4, zz, c), place((y + 1) % 4, zz, c), csend.at[k, 2], crecv.at[k, 2], sibling).start()
    for k in (0, 1, 3, 2):
        zz = (z + 4 - k) % 4
        far = (y + 2) % 4
        remote(place(far, zz, c, 0, cut), place(far, zz, c, 0, cut), ysend.at[k, 2], yrecv.at[k, 2], at_y(1)).wait_recv()
        remote(place(far, zz, c, cut, SEED - cut), place(far, zz, c, cut, SEED - cut), ysend.at[k, 3], yrecv.at[k, 3], at_y(3)).wait_recv()
        remote(place(far, zz, c), place(far, zz, c), csend.at[k, 3], crecv.at[k, 3], sibling).start()
    for k in range(4):
        for j in range(4):
            remote(s_ref, place(y, z, 1 - c), csend.at[k, j], crecv.at[k, j], sibling).wait()
        for j, n in ((0, SEED), (1, SEED), (2, cut), (3, SEED - cut)):
            remote(s_ref.at[pl.ds(0, n)], place(y, z, c, 0, n), ysend.at[k, j], yrecv.at[k, j], sibling).wait_send()
    for s in zs:
        s.wait_send()
    keep.wait()
    for s in ws:
        s.wait_send()
    rows = pl.ds(0, HROWS)
    for j in range(2):
        remote(w_ref.at[rows], wg_ref.at[1, rows], wsend.at[0], wrecv.at[1, j], sibling).wait_recv()

    @pl.when(c == 0)
    def _():
        keep_w.wait()

    @pl.when(c == 1)
    def _():
        for j in range(2):
            remote(w_ref.at[rows], wg_ref.at[0, rows], wsend.at[0], wrecv.at[0, j], sibling).wait_recv()

    for k in range(2):
        to = 2 * c + k
        mine = (x == to) & (c == 0)

        @pl.when(mine)
        def _():
            keep_d.wait()

        @pl.when(jnp.logical_not(mine))
        def _():
            remote(d_ref.at[0], dg_ref.at[0], dsend.at[k], drecv.at[0], sibling).wait_send()

    here = (c == 0) & (x // 2 == 0)

    @pl.when(jnp.logical_not(here))
    def _():
        remote(d_ref.at[0], dg_ref.at[0], dsend.at[0], drecv.at[0], sibling).wait_recv()

    remote(d_ref.at[0], dg_ref.at[1], dsend.at[0], drecv.at[1], sibling).wait_recv()


def partial_kernel(p_ref, r_ref, send, recv, local):
    zh, c, y, x, z = where_am_i()
    sibling = device(zh, 1 - c, y, x, z)
    barrier([sibling] + [device(zh, k, y, (x + q) % 4, z) for q in range(1, 4) for k in range(2)])
    for k in range(2):
        d = 2 * c + k
        to = (x + d) % 4
        for j in range(2):
            src = p_ref.at[k, pl.ds(j * HROWS, HROWS)]
            mine = (d == 0) & (c == j)

            @pl.when(mine)
            def _():
                pltpu.make_async_copy(src, r_ref.at[x], local).start()

            @pl.when(jnp.logical_not(mine))
            def _():
                remote(src, r_ref.at[x], send.at[k, j], recv.at[(4 - d) % 4], device(zh, j, y, to, z)).start()
    for k in range(2):
        d = 2 * c + k
        for j in range(2):
            src = p_ref.at[k, pl.ds(j * HROWS, HROWS)]
            mine = (d == 0) & (c == j)

            @pl.when(mine)
            def _():
                pltpu.make_async_copy(src, r_ref.at[x], local).wait()

            @pl.when(jnp.logical_not(mine))
            def _():
                remote(src, r_ref.at[x], send.at[k, j], recv.at[0], sibling).wait_send()

    for q in range(1, 4):
        remote(p_ref.at[0, pl.ds(0, HROWS)], r_ref.at[0], send.at[0, 0], recv.at[q], sibling).wait_recv()

    @pl.when(c == 1)
    def _():
        remote(p_ref.at[0, pl.ds(0, HROWS)], r_ref.at[0], send.at[0, 0], recv.at[0], sibling).wait_recv()


def halves_kernel(s_ref, t_ref, send, recv, local):
    zh, c, y, x, z = where_am_i()
    sibling, far = device(zh, 1 - c, y, x, z), device(1 - zh, c, y, x, z)
    barrier([sibling, far])
    over = remote(s_ref, t_ref.at[c, zh], send.at[0], recv.at[0], far)
    over.start()
    beside = remote(s_ref, t_ref.at[c, zh], send.at[1], recv.at[1], sibling)
    beside.start()
    keep = pltpu.make_async_copy(s_ref, t_ref.at[c, zh], local)
    keep.start()
    over.wait_recv()
    after = remote(t_ref.at[c, 1 - zh], t_ref.at[c, 1 - zh], send.at[2], recv.at[2], sibling)
    after.start()
    keep.wait()
    over.wait_send()
    beside.wait()
    after.wait()


def params(k):
    return pltpu.CompilerParams(collective_id=k, has_side_effects=True)


DMA = pltpu.SemaphoreType.DMA


def per_device(features, cotangent, up_rows, moment, exponents):
    bf16 = jnp.bfloat16
    seeds = pl.pallas_call(
        seed_kernel,
        out_shape=jax.ShapeDtypeStruct((2, TOK, HALF), bf16),
        in_specs=[ANY], out_specs=ANY,
        scratch_shapes=[DMA((2,)), DMA((2,)), DMA],
        compiler_params=params(0), name="seeds",
    )(features)
    seeds = seeds.reshape(SEED, HALF)
    dy = cotangent.reshape(4, 4, 4, TOK, ROWS)
    dy = jnp.stack([jnp.stack([dy[:, a], dy[:, b]], axis=2) for a, b in ((0, 3), (1, 2))])
    dy = dy.reshape(2, CLASS_TOK, ROWS)
    x, w, dy = pl.pallas_call(
        gather_kernel,
        out_shape=[jax.ShapeDtypeStruct((CLASS_TOK, D), bf16), jax.ShapeDtypeStruct((2, ROWS, D), bf16), jax.ShapeDtypeStruct((2, CLASS_TOK, ROWS), bf16)],
        in_specs=[ANY] * 3, out_specs=[ANY] * 3,
        scratch_shapes=[DMA((4,)), DMA((4,)), DMA((4, 4)), DMA((4, 4)), DMA((4, 4)), DMA((4, 4)), DMA((4,)), DMA((2, 2)), DMA((2,)), DMA((2,)), DMA((3,))],
        compiler_params=params(1), name="gather",
    )(seeds, up_rows, dy)
    parts = []
    for k in range(2):
        preact = jnp.einsum("td,fd->tf", x, w[k], preferred_element_type=jnp.float32)
        s = jax.nn.sigmoid(preact)
        hidden = (dy[k].astype(jnp.float32) * (s * (1.0 + preact * (1.0 - s)))).astype(bf16)
        parts.append(jnp.einsum("tf,td->fd", hidden, x, preferred_element_type=jnp.float32).astype(bf16))
    part = jnp.stack(parts)
    got = pl.pallas_call(
        partial_kernel,
        out_shape=jax.ShapeDtypeStruct((4, HROWS, D), bf16),
        in_specs=[ANY], out_specs=ANY,
        scratch_shapes=[DMA((2, 2)), DMA((4,)), DMA],
        compiler_params=params(2), name="partials",
    )(part)
    c = lax.axis_index("rep") % 2
    power = exponents.astype(jnp.float32)
    mine = lax.dynamic_slice_in_dim(power, c * HROWS, HROWS, 0)[:, :, None]
    got = got.astype(jnp.float32).reshape(4, HROWS, D // 128, 128) * jnp.exp2(-mine)
    coded = [jnp.clip(inner_rate * (got[2 * g] + got[2 * g + 1]), -code_limit, code_limit).astype(bf16).astype(jnp.float32) for g in range(2)]
    both = (coded[0] + coded[1]).astype(bf16).reshape(HROWS, D)
    terms = pl.pallas_call(
        halves_kernel,
        out_shape=jax.ShapeDtypeStruct((2, 2, HROWS, D), bf16),
        in_specs=[ANY], out_specs=ANY,
        scratch_shapes=[DMA((3,)), DMA((3,)), DMA],
        compiler_params=params(3), name="halves",
    )(both)
    terms = terms.astype(jnp.float32)
    summed = (terms[:, 0] + terms[:, 1]).reshape(ROWS, D // 128, 128)
    decoded = (summed * jnp.exp2(power)[:, :, None]).reshape(ROWS, D) / 4.0
    new_moment = momentum_coef * moment + decoded
    new_params = (up_rows.astype(jnp.float32) - outer_rate * (decoded + momentum_coef * new_moment)).astype(bf16)
    return new_params, new_moment


def solution(mesh):
    return jax.shard_map(
        per_device,
        mesh=mesh,
        in_specs=(P(("rep", "fsdp"), None), P("rep", "fsdp"), P("fsdp", None), P("fsdp", None), P("fsdp", None)),
        out_specs=(P("fsdp", None), P("fsdp", None)),
        check_vma=False,
    )
```

```python
import functools

import jax
import jax.numpy as jnp
from jax import lax
from jax.experimental import pallas as pl
from jax.experimental.pallas import tpu as pltpu
from jax.sharding import PartitionSpec as P

inner_rate = 0.02
outer_rate = 0.7
momentum_coef = 0.9
code_limit = 448.0

D = 4096
HALF = D // 2
TOK = 56
SEED = 2 * TOK
CLASS_TOK = 1792
ROWS = 224
HROWS = ROWS // 2
TILE = 512
TILES = D // TILE
MESH = pl.DeviceIdType.MESH
ANY = pl.BlockSpec(memory_space=pl.ANY)


def where_am_i():
    rep, at = lax.axis_index("rep"), lax.axis_index("fsdp")
    return rep // 2, rep % 2, at // 16, (at // 4) % 4, at % 4


def device(zh, c, y, x, z):
    return (zh * 2 + c, (y * 4 + x) * 4 + z)


def barrier(peers):
    sem = pltpu.get_barrier_semaphore()
    for peer in peers:
        pl.semaphore_signal(sem, inc=1, device_id=peer, device_id_type=MESH)
    pl.semaphore_wait(sem, len(peers))


def remote(src, dst, send_sem, recv_sem, peer):
    return pltpu.make_async_remote_copy(src, dst, send_sem, recv_sem, device_id=peer, device_id_type=MESH)


def slope(p):
    s = jax.nn.sigmoid(p)
    return s * (1.0 + p * (1.0 - s))


def work_kernel(f_ref, w_ref, d_ref, m_ref, e_ref, np_ref, nm_ref,
                xs, seed, wv, dv, acc, pre, ht, got, terms, mom, rows_in, rows_out, up, down,
                seed_send, seed_recv, zsend, zrecv, ysend, yrecv, csend, crecv, wsend, wrecv, dsend, drecv, local,
                psend, precv, plocal, fsend, frecv, bsend, brecv, out):
    zh, c, y, x, z = where_am_i()

    def at_y(k):
        return device(zh, c, (y + k) % 4, x, z)

    sibling = device(zh, 1 - c, y, x, z)
    peers = [sibling, at_y(1), at_y(3)]
    peers += [device(zh, c, y, x, (z + k) % 4) for k in range(1, 4)]
    peers += [device(zh, k, y, (x + q) % 4, z) for q in range(1, 4) for k in range(2)]
    keep_w = pltpu.make_async_copy(w_ref, wv.at[pl.ds(0, ROWS)], local.at[1])

    @pl.when(c == 0)
    def _():
        keep_w.start()

    other_half = device(1 - zh, c, y, x, z)
    barrier(peers + [other_half])
    loads = [pltpu.make_async_copy(m_ref, mom, local.at[4]), pltpu.make_async_copy(w_ref, rows_in, local.at[5])]
    for load in loads:
        load.start()

    mirror = 3 - x
    slot = x // 2
    whole = f_ref.at[:, pl.ds(0, HALF)]

    def half(k):
        return f_ref.at[:, pl.ds(pl.multiple_of(k * HALF, HALF), HALF)]

    @pl.when(c == slot)
    def _():
        keep = pltpu.make_async_copy(half(c), seed.at[slot], local.at[0])
        give = remote(half(1 - c), seed.at[slot], seed_send.at[0], seed_recv.at[slot], sibling)
        keep.start()
        give.start()
        keep.wait()
        give.wait_send()
        remote(whole, seed.at[1 - slot], seed_send.at[0], seed_recv.at[1 - slot], sibling).wait_recv()

    @pl.when(c != slot)
    def _():
        sends = [remote(half(k), seed.at[slot], seed_send.at[k], seed_recv.at[slot], device(zh, k, y, mirror, z)) for k in range(2)]
        for s in sends:
            s.start()
        for s in sends:
            s.wait_send()
        for k in range(2):
            remote(whole, seed.at[k], seed_send.at[0], seed_recv.at[k], sibling).wait_recv()

    def place(yy, zz, core, lo=0, n=SEED):
        return xs.at[core, pl.ds(pl.multiple_of((yy * 4 + zz) * SEED + lo, 16), n)]

    joined = jnp.concatenate([seed[0].astype(jnp.float32), seed[1].astype(jnp.float32)], axis=0)
    xs[c, pl.ds(pl.multiple_of((y * 4 + z) * SEED, 16), SEED), :] = joined.astype(jnp.bfloat16)
    own = place(y, z, c)

    zs = [remote(own, own, zsend.at[k], zrecv.at[k], device(zh, c, y, x, (z + k) % 4)) for k in range(1, 4)]
    for s in zs:
        s.start()

    def pass_on(k, zz):
        src = place(y, zz, c)
        remote(src, src, ysend.at[k, 0], yrecv.at[k, 0], at_y(1)).start()
        remote(src, src, ysend.at[k, 1], yrecv.at[k, 1], at_y(3)).start()
        remote(src, src, csend.at[k, 0], crecv.at[k, 0], sibling).start()

    pass_on(0, z)

    ws = []
    for d in range(1, 4):
        src = w_ref.at[pl.ds(pl.multiple_of(c * HROWS, 16), HROWS)]
        dst = wv.at[pl.ds(pl.multiple_of((d % 2) * ROWS + c * HROWS, 16), HROWS)]
        ws.append(remote(src, dst, wsend.at[d], wrecv.at[d % 2, c], device(zh, d // 2, y, (x + 4 - d) % 4, z)))
    for s in ws:
        s.start()

    def dy_of(k):
        to = 2 * c + k
        d = (x - to + 4) % 4
        outer = (to == 0) | (to == 3)
        sets = [jnp.where(outer, 0, 1), jnp.where(outer, 3, 2)]
        return to, d, sets, (d == 0) & (c == 0)

    for k in range(2):
        to, d, sets, mine = dy_of(k)
        for i in range(2):
            @pl.when(mine)
            def _():
                pltpu.make_async_copy(d_ref.at[:, sets[i]], dv.at[0, i], local.at[2 + i]).start()

            @pl.when(jnp.logical_not(mine))
            def _():
                remote(d_ref.at[:, sets[i]], dv.at[d % 2, i], dsend.at[k, i], drecv.at[d % 2, i], device(zh, d // 2, y, to, z)).start()

    def wait_w_and_dy():
        rows = pl.ds(0, HROWS)
        for j in range(2):
            remote(w_ref.at[rows], wv.at[rows], wsend.at[0], wrecv.at[1, j], sibling).wait_recv()

        @pl.when(c == 0)
        def _():
            keep_w.wait()

        @pl.when(c == 1)
        def _():
            for j in range(2):
                remote(w_ref.at[rows], wv.at[rows], wsend.at[0], wrecv.at[0, j], sibling).wait_recv()

        here = (c == 0) & (x // 2 == 0)
        for i in range(2):
            @pl.when(here)
            def _():
                pltpu.make_async_copy(d_ref.at[:, 0], dv.at[0, i], local.at[2 + i]).wait()

            @pl.when(jnp.logical_not(here))
            def _():
                remote(d_ref.at[:, 0], dv.at[0, i], dsend.at[0, i], drecv.at[0, i], sibling).wait_recv()

            remote(d_ref.at[:, 0], dv.at[1, i], dsend.at[0, i], drecv.at[1, i], sibling).wait_recv()

    cut = 64

    def forward(k):
        zz = (z + 4 - k) % 4
        up, down = (y + 3) % 4, (y + 1) % 4
        remote(own, place(up, zz, c), ysend.at[k, 0], yrecv.at[k, 0], at_y(1)).wait_recv()
        src = place(up, zz, c, 0, cut)
        remote(src, src, ysend.at[k, 2], yrecv.at[k, 2], at_y(1)).start()
        src = place(up, zz, c)
        remote(src, src, csend.at[k, 1], crecv.at[k, 1], sibling).start()
        remote(own, place(down, zz, c), ysend.at[k, 1], yrecv.at[k, 1], at_y(3)).wait_recv()
        src = place(down, zz, c, cut, SEED - cut)
        remote(src, src, ysend.at[k, 3], yrecv.at[k, 3], at_y(3)).start()
        src = place(down, zz, c)
        remote(src, src, csend.at[k, 2], crecv.at[k, 2], sibling).start()

    def from_sibling(j):
        for k in range(4):
            remote(own, own, csend.at[k, j], crecv.at[k, j], sibling).wait_recv()

    def partial_parts(t):
        for k in range(2):
            d = 2 * c + k
            src = wv.at[pl.ds(k * ROWS, ROWS), pl.ds(pl.multiple_of(t * TILE, TILE), TILE)]
            to = device(zh, t % 2, y, (x + d) % 4, z)
            yield k, d, src, to, (d == 0) & (c == t % 2)

    def send_partials(t):
        for k, d, src, to, mine in partial_parts(t):
            @pl.when(mine)
            def _():
                pltpu.make_async_copy(src, got.at[t // 2, x], plocal.at[t // 2]).start()

            @pl.when(jnp.logical_not(mine))
            def _():
                remote(src, got.at[t // 2, x], psend.at[k, t], precv.at[t // 2, (4 - d) % 4], to).start()

    def compute(yy, first, last):
        rows = pl.ds(pl.multiple_of(yy * 448, 448), 448)
        pre[...] = jnp.zeros_like(pre)
        for h in range(2):
            @pl.loop(0, 4)
            def _(t):
                cols = pl.ds(pl.multiple_of(t * 512, 512), 512)
                wide = pl.ds(pl.multiple_of(h * HALF + t * 512, 512), 512)
                xt = xs[h, rows, cols]
                for k in range(2):
                    wt = wv[pl.ds(k * ROWS, ROWS), wide]
                    pre[k] += lax.dot_general(xt, wt, (((1,), (1,)), ((), ())), preferred_element_type=jnp.float32)
        for k in range(2):
            dy = [dv[k, i, yy].astype(jnp.float32) for i in range(2)]
            dy = jnp.concatenate([dy[i][zz * TOK:(zz + 1) * TOK] for zz in range(4) for i in range(2)], axis=0)
            hid = dy * slope(pre[k])
            ht[pl.ds(k * ROWS, ROWS), :] = hid.T.astype(jnp.bfloat16)
        for h in range(2):
            @pl.loop(0, 4)
            def _(t):
                cols = pl.ds(pl.multiple_of(t * 512, 512), 512)
                wide = pl.ds(pl.multiple_of(h * HALF + t * 512, 512), 512)
                g = jnp.dot(ht[...], xs[h, rows, cols], preferred_element_type=jnp.float32)
                if not first:
                    g = g + acc[:, wide]
                if not last:
                    acc[:, wide] = g
                else:
                    wv[:, wide] = g.astype(jnp.bfloat16)
                    send_partials(h * 4 + t)

    power = e_ref[...].astype(jnp.float32)
    bigger, smaller = jnp.exp2(power), jnp.exp2(-power)
    for b in range(D // 128):
        cols = pl.ds(b * 128, 128)
        up[:, cols] = jnp.broadcast_to(bigger[:, b:b + 1], (ROWS, 128)).astype(jnp.bfloat16)
        down[:, cols] = jnp.broadcast_to(smaller[:, b:b + 1], (ROWS, 128)).astype(jnp.bfloat16)

    for k in (1, 3, 2):
        remote(own, own, zsend.at[k], zrecv.at[k], sibling).wait_recv()
        pass_on(k, (z + 4 - k) % 4)
    forward(0)
    forward(1)
    wait_w_and_dy()
    from_sibling(0)
    compute(y, True, False)
    forward(3)
    forward(2)
    from_sibling(1)
    compute((y + 3) % 4, False, False)
    for k in (0, 1, 3, 2):
        zz = (z + 4 - k) % 4
        far = (y + 2) % 4
        src = place(far, zz, c, 0, cut)
        remote(src, src, ysend.at[k, 2], yrecv.at[k, 2], at_y(1)).wait_recv()
        src = place(far, zz, c, cut, SEED - cut)
        remote(src, src, ysend.at[k, 3], yrecv.at[k, 3], at_y(3)).wait_recv()
        src = place(far, zz, c)
        remote(src, src, csend.at[k, 3], crecv.at[k, 3], sibling).start()
    from_sibling(2)
    compute((y + 1) % 4, False, False)
    from_sibling(3)
    for k in range(4):
        for j in range(4):
            remote(own, own, csend.at[k, j], crecv.at[k, j], sibling).wait_send()
        for j, n in ((0, SEED), (1, SEED), (2, cut), (3, SEED - cut)):
            src = place(y, z, c, 0, n)
            remote(src, src, ysend.at[k, j], yrecv.at[k, j], sibling).wait_send()
    for s in zs + ws:
        s.wait_send()
    for k in range(2):
        to, d, sets, mine = dy_of(k)
        for i in range(2):
            @pl.when(jnp.logical_not(mine))
            def _():
                remote(d_ref.at[:, 0], dv.at[0, i], dsend.at[k, i], drecv.at[0, i], sibling).wait_send()
    compute((y + 2) % 4, False, True)
    piece = wv.at[pl.ds(0, ROWS), pl.ds(0, TILE)]
    owned = got.at[0, 0]
    crossing = []
    for i in range(TILES // 2):
        t = 2 * i + c
        cols = pl.ds(pl.multiple_of(t * TILE, TILE), TILE)
        for q in range(1, 4):
            remote(piece, owned, psend.at[0, 0], precv.at[i, q], sibling).wait_recv()

        @pl.when(c == 0)
        def _():
            pltpu.make_async_copy(piece, owned, plocal.at[i]).wait()

        @pl.when(c == 1)
        def _():
            remote(piece, owned, psend.at[0, 0], precv.at[i, 0], sibling).wait_recv()

        shrink = down[:, cols].astype(jnp.float32)

        def coded(g):
            total = got[i, 2 * g].astype(jnp.float32) + got[i, 2 * g + 1].astype(jnp.float32)
            return jnp.clip(inner_rate * (total * shrink), -code_limit, code_limit).astype(jnp.bfloat16).astype(jnp.float32)

        terms[t, zh] = (coded(0) + coded(1)).astype(jnp.bfloat16)
        here = terms.at[t, zh]
        over = remote(here, here, fsend.at[i], frecv.at[i], other_half)
        beside = remote(here, here, bsend.at[i, 0], brecv.at[i, 0], sibling)
        over.start()
        beside.start()
        crossing += [over, beside]
    for load in loads:
        load.wait()

    def finish(t, slot):
        cols = pl.ds(pl.multiple_of(t * TILE, TILE), TILE)
        total = terms[t, 0].astype(jnp.float32) + terms[t, 1].astype(jnp.float32)
        decoded = total * up[:, cols].astype(jnp.float32) / 4.0
        new_moment = momentum_coef * mom[:, cols] + decoded
        mom[:, cols] = new_moment
        rows_out[:, cols] = (rows_in[:, cols].astype(jnp.float32) - outer_rate * (decoded + momentum_coef * new_moment)).astype(jnp.bfloat16)
        writes = [pltpu.make_async_copy(mom.at[:, cols], nm_ref.at[:, cols], out.at[slot, 0]),
                  pltpu.make_async_copy(rows_out.at[:, cols], np_ref.at[:, cols], out.at[slot, 1])]
        for write in writes:
            write.start()
        return writes

    writes = []
    for i in range(TILES // 2):
        t, u = 2 * i + c, 2 * i + 1 - c
        remote(owned, owned, fsend.at[i], frecv.at[i], other_half).wait_recv()
        there = terms.at[t, 1 - zh]
        after = remote(there, there, bsend.at[i, 1], brecv.at[i, 1], sibling)
        after.start()
        crossing.append(after)
        writes += finish(t, 2 * i)
        for j in range(2):
            remote(owned, owned, bsend.at[i, j], brecv.at[i, j], sibling).wait_recv()
        writes += finish(u, 2 * i + 1)
    for s in crossing:
        s.wait_send()
    for t in range(TILES):
        for k, d, src, to, mine in partial_parts(t):
            @pl.when(jnp.logical_not(mine))
            def _():
                remote(src, owned, psend.at[k, t], precv.at[0, 0], sibling).wait_send()
    for write in writes:
        write.wait()


DMA = pltpu.SemaphoreType.DMA


def per_device(features, cotangent, up_rows, moment, exponents):
    bf16 = jnp.bfloat16
    dy = cotangent.reshape(4, 4, ROWS, ROWS)
    f32 = jnp.float32
    return pl.pallas_call(
        work_kernel,
        out_shape=[jax.ShapeDtypeStruct((ROWS, D), bf16), jax.ShapeDtypeStruct((ROWS, D), f32)],
        in_specs=[ANY] * 4 + [pl.BlockSpec(memory_space=pltpu.VMEM)], out_specs=[ANY] * 2,
        scratch_shapes=[
            pltpu.VMEM((2, CLASS_TOK, HALF), bf16), pltpu.VMEM((2, TOK, HALF), bf16), pltpu.VMEM((2 * ROWS, D), bf16),
            pltpu.VMEM((2, 2, 4, ROWS, ROWS), bf16), pltpu.VMEM((2 * ROWS, D), f32),
            pltpu.VMEM((2, 448, ROWS), f32), pltpu.VMEM((2 * ROWS, 448), bf16),
            pltpu.VMEM((TILES // 2, 4, ROWS, TILE), bf16), pltpu.VMEM((TILES, 2, ROWS, TILE), bf16),
            pltpu.VMEM((ROWS, D), f32), pltpu.VMEM((ROWS, D), bf16), pltpu.VMEM((ROWS, D), bf16),
            pltpu.VMEM((ROWS, D), bf16), pltpu.VMEM((ROWS, D), bf16),
            DMA((2,)), DMA((2,)), DMA((4,)), DMA((4,)), DMA((4, 4)), DMA((4, 4)), DMA((4, 4)), DMA((4, 4)),
            DMA((4,)), DMA((2, 2)), DMA((2, 2)), DMA((2, 2)), DMA((6,)),
            DMA((2, TILES)), DMA((TILES // 2, 4)), DMA((TILES // 2,)), DMA((TILES // 2,)), DMA((TILES // 2,)),
            DMA((TILES // 2, 2)), DMA((TILES // 2, 2)), DMA((TILES, 2))],
        compiler_params=pltpu.CompilerParams(collective_id=0, has_side_effects=True, vmem_limit_bytes=60 * 2**20), name="work",
    )(features, up_rows, dy, moment, exponents)


def solution(mesh):
    return jax.shard_map(
        per_device,
        mesh=mesh,
        in_specs=(P(("rep", "fsdp"), None), P("rep", "fsdp"), P("fsdp", None), P("fsdp", None), P("fsdp", None)),
        out_specs=(P("fsdp", None), P("fsdp", None)),
        check_vma=False,
    )
```

```python
import functools

import jax
import jax.numpy as jnp
from jax import lax
from jax.experimental import pallas as pl
from jax.experimental.pallas import tpu as pltpu
from jax.sharding import PartitionSpec as P

inner_rate = 0.02
outer_rate = 0.7
momentum_coef = 0.9
code_limit = 448.0

D = 4096
HALF = D // 2
TOK = 56
SEED = 2 * TOK
LATE = 16
SOON = SEED - LATE
WIDE = 1024
TOKENS = 3584
ROWS = 224
HROWS = ROWS // 2
TILE = 256
TILES = D // TILE
MESH = pl.DeviceIdType.MESH
ANY = pl.BlockSpec(memory_space=pl.ANY)


def where_am_i():
    rep, at = lax.axis_index("rep"), lax.axis_index("fsdp")
    return rep // 2, rep % 2, at // 16, (at // 4) % 4, at % 4


def device(zh, c, y, x, z):
    return (zh * 2 + c, (y * 4 + x) * 4 + z)


def barrier(peers):
    sem = pltpu.get_barrier_semaphore()
    for peer in peers:
        pl.semaphore_signal(sem, inc=1, device_id=peer, device_id_type=MESH)
    pl.semaphore_wait(sem, len(peers))


def remote(src, dst, send_sem, recv_sem, peer):
    return pltpu.make_async_remote_copy(src, dst, send_sem, recv_sem, device_id=peer, device_id_type=MESH)


def slope(p):
    s = jax.nn.sigmoid(p)
    return s * (1.0 + p * (1.0 - s))


def work_kernel(f_ref, w_ref, d_ref, m_ref, e_ref, np_ref, nm_ref,
                xs, seed, wv, dv, acc, pre, ht, got, terms, mom, rows_in, rows_out, up, down, dt, turned, dn,
                seed_send, seed_recv, zsend, zrecv, ysend, yrecv, csend, crecv, lysend, lyrecv, lzsend, lzrecv, lcsend, lcrecv, wsend, wrecv, dsend, drecv, dlocal, local,
                psend, precv, plocal, fsend, frecv, bsend, brecv, out):
    zh, c, y, x, z = where_am_i()

    def at_y(k):
        return device(zh, c, (y + k) % 4, x, z)

    sibling = device(zh, 1 - c, y, x, z)
    peers = [sibling, at_y(1), at_y(3)]
    peers += [device(zh, c, y, x, (z + k) % 4) for k in range(1, 4)]
    peers += [device(zh, k, y, (x + q) % 4, z) for q in range(1, 4) for k in range(2)]
    keep_w = pltpu.make_async_copy(w_ref, wv.at[pl.ds(0, ROWS)], local.at[1])

    load_d = pltpu.make_async_copy(d_ref, dt, local.at[0])
    load_d.start()

    @pl.when(c == 0)
    def _():
        keep_w.start()

    other_half = device(1 - zh, c, y, x, z)
    barrier(peers + [other_half])
    loads = [pltpu.make_async_copy(m_ref, mom, local.at[4]), pltpu.make_async_copy(w_ref, rows_in, local.at[5])]
    for load in loads:
        load.start()

    mirror = 3 - x
    slot = x // 2
    whole = f_ref.at[:, pl.ds(0, HALF)]

    def half(k):
        return f_ref.at[:, pl.ds(pl.multiple_of(k * HALF, HALF), HALF)]

    keep = pltpu.make_async_copy(half(c), seed.at[slot], local.at[6])
    give = remote(half(1 - c), seed.at[slot], seed_send.at[0], seed_recv.at[slot], sibling)
    across = [remote(half(k), seed.at[slot], seed_send.at[k], seed_recv.at[slot], device(zh, k, y, mirror, z)) for k in range(2)]

    @pl.when(c == slot)
    def _():
        keep.start()
        give.start()

    @pl.when(c != slot)
    def _():
        for s in across:
            s.start()

    near = []
    for k in range(2):
        src = w_ref.at[pl.ds(pl.multiple_of(c * HROWS, 16), HROWS)]
        dst = wv.at[pl.ds(pl.multiple_of((1 - k) * ROWS + c * HROWS, 16), HROWS)]
        near.append(remote(src, dst, wsend.at[k], wrecv.at[1 - k, c], device(zh, k, y, (x + 3 + 2 * k) % 4, z)))

    for k in range(2):
        @pl.when(x % 2 != k)
        def _():
            near[k].start()

    load_d.wait()
    for b in range(TOKENS // 256):
        turned[pl.ds(b * 256, 256), :] = dt[:, pl.ds(b * 256, 256)].astype(jnp.float32).T

    @pl.when(c == slot)
    def _():
        keep.wait()
        give.wait_send()
        remote(whole, seed.at[1 - slot], seed_send.at[0], seed_recv.at[1 - slot], sibling).wait_recv()

    @pl.when(c != slot)
    def _():
        for s in across:
            s.wait_send()
        for k in range(2):
            remote(whole, seed.at[k], seed_send.at[0], seed_recv.at[k], sibling).wait_recv()

    def place(yy, zz, core, lo=0, n=SOON):
        return xs.at[core, zz, yy, pl.ds(lo, n)]

    joined = jnp.concatenate([seed[0].astype(jnp.float32), seed[1].astype(jnp.float32)], axis=0)
    xs[c, z, y] = joined.astype(jnp.bfloat16)
    own = place(y, z, c)

    inner = (z == 1) | (z == 2)
    order = [z, z + 1 - 2 * (z % 2), jnp.where(z < 2, 2, 1), jnp.where(z < 2, 3, 0)]

    def at_z(zz):
        return device(zh, c, y, x, zz)

    @pl.when(z < 3)
    def _():
        remote(own, own, zsend.at[0], zrecv.at[z], at_z(z + 1)).start()

    @pl.when(z > 0)
    def _():
        remote(own, own, zsend.at[1], zrecv.at[z], at_z(z - 1)).start()

    def pass_on(n):
        zz = order[n]
        src = place(y, zz, c)
        remote(src, src, ysend.at[n, 0], yrecv.at[zz, 0], at_y(1)).start()
        remote(src, src, ysend.at[n, 1], yrecv.at[zz, 1], at_y(3)).start()
        remote(src, src, csend.at[n, 0], crecv.at[zz, 0], sibling).start()

    def from_z(n):
        src = place(y, order[n], c)
        remote(src, src, zsend.at[1 + n], zrecv.at[order[n]], sibling).wait_recv()

        @pl.when(inner)
        def _():
            to = 3 - z if n == 1 else jnp.where(z == 1, 0, 3)
            remote(src, src, zsend.at[1 + n], zrecv.at[order[n]], at_z(to)).start()

        pass_on(n)

    def late(yy, k=None):
        if k is None:
            return xs.at[c, z, yy, pl.ds(SOON, LATE)]
        return xs.at[c, z, yy, pl.ds(SOON, LATE), pl.ds(k * (HALF // 2), HALF // 2)]

    def late_y(j):
        src = [late(y), late(y), late((y + 3) % 4, 0), late((y + 1) % 4, 1)][j]
        return remote(src, src, lysend.at[j], lyrecv.at[j], at_y(1 if j % 2 == 0 else 3))

    def late_block(zz):
        return xs.at[c, zz, :, pl.ds(SOON, LATE)]

    def late_z(k, zz, to):
        return remote(late_block(zz), late_block(zz), lzsend.at[k], lzrecv.at[zz], to)

    def late_share(n):
        src = late_block(order[n])
        remote(src, src, lcsend.at[n], lcrecv.at[order[n]], sibling).start()

    def late_from_z(n):
        late_z(1 + n, order[n], sibling).wait_recv()

        @pl.when(inner)
        def _():
            late_z(1 + n, order[n], at_z(3 - z if n == 1 else jnp.where(z == 1, 0, 3))).start()

        late_share(n)

    late_y(0).start()
    late_y(1).start()
    pass_on(0)

    def w_forward():
        row = (1 - c) * HROWS
        src = wv.at[pl.ds(pl.multiple_of((1 - c) * ROWS + row, 16), HROWS)]
        dst = wv.at[pl.ds(pl.multiple_of(ROWS + row, 16), HROWS)]
        return remote(src, dst, wsend.at[2], wrecv.at[1, 1 - c], device(zh, 1, y, (x + 3 + 2 * c) % 4, z))

    def forward_w():
        remote(w_ref.at[pl.ds(0, HROWS)], wv.at[pl.ds(0, HROWS)], wsend.at[2], wrecv.at[1 - c, 1 - c], sibling).wait_recv()
        w_forward().start()

    def wait_w():
        def arrived(k, j):
            remote(w_ref.at[pl.ds(0, HROWS)], wv.at[pl.ds(0, HROWS)], wsend.at[2], wrecv.at[k, j], sibling).wait_recv()

        arrived(1 - c, c)

        @pl.when(c == 0)
        def _():
            keep_w.wait()

        @pl.when(c == 1)
        def _():
            arrived(1, 0)
            arrived(1, 1)

    def make_dy(zz):
        for h, pair in enumerate(((0, 3), (1, 2))):
            for yy in range(4):
                both = [turned[pl.ds(pl.multiple_of(((yy * 4 + at) * 4 + zz) * TOK, 8), TOK), :] for at in pair]
                dn[h, zz, yy] = jnp.concatenate(both, axis=0).astype(jnp.bfloat16)

    def dy_parts(zz):
        for k in range(2):
            to = 2 * c + k
            d = (x - to + 4) % 4
            h = jnp.where((to == 0) | (to == 3), 0, 1)
            yield dn.at[h, zz], (d + d // 2) % 2, device(zh, d // 2, y, to, z), k, (d == 0) & (c == 0)

    def send_dy(zz):
        for src, slot_to, to, k, mine in dy_parts(zz):
            @pl.when(mine)
            def _():
                pltpu.make_async_copy(src, dv.at[0, zz], dlocal.at[zz]).start()

            @pl.when(jnp.logical_not(mine))
            def _():
                remote(src, dv.at[slot_to, zz], dsend.at[k, zz], drecv.at[slot_to, zz], to).start()

    def wait_dy(zz):
        here = (c == 0) & (x // 2 == 0)

        @pl.when(here)
        def _():
            pltpu.make_async_copy(dn.at[0, zz], dv.at[0, zz], dlocal.at[zz]).wait()

        @pl.when(jnp.logical_not(here))
        def _():
            remote(dn.at[0, zz], dv.at[0, zz], dsend.at[0, zz], drecv.at[0, zz], sibling).wait_recv()

        remote(dn.at[0, zz], dv.at[1, zz], dsend.at[0, zz], drecv.at[1, zz], sibling).wait_recv()

    for k in range(2):
        @pl.when(x % 2 == k)
        def _():
            near[k].start()

    make_dy(order[0])
    for j in range(2):
        late_y(j).wait_recv()
        late_y(2 + j).start()

    cut = SOON // 2

    def forward(n):
        zz = order[n]
        above, below = (y + 3) % 4, (y + 1) % 4
        remote(own, place(above, zz, c), ysend.at[n, 0], yrecv.at[zz, 0], at_y(1)).wait_recv()
        src = place(above, zz, c, 0, cut)
        remote(src, src, ysend.at[n, 2], yrecv.at[zz, 2], at_y(1)).start()
        src = place(above, zz, c)
        remote(src, src, csend.at[n, 1], crecv.at[zz, 1], sibling).start()
        remote(own, place(below, zz, c), ysend.at[n, 1], yrecv.at[zz, 1], at_y(3)).wait_recv()
        src = place(below, zz, c, cut, SOON - cut)
        remote(src, src, ysend.at[n, 3], yrecv.at[zz, 3], at_y(3)).start()
        src = place(below, zz, c)
        remote(src, src, csend.at[n, 2], crecv.at[zz, 2], sibling).start()

    def from_far(n):
        zz, far = order[n], (y + 2) % 4
        src = place(far, zz, c, 0, cut)
        remote(src, src, ysend.at[n, 2], yrecv.at[zz, 2], at_y(1)).wait_recv()
        src = place(far, zz, c, cut, SOON - cut)
        remote(src, src, ysend.at[n, 3], yrecv.at[zz, 3], at_y(3)).wait_recv()
        src = place(far, zz, c)
        remote(src, src, csend.at[n, 3], crecv.at[zz, 3], sibling).start()

    def from_sibling(n):
        for j in range(4):
            remote(own, own, csend.at[n, j], crecv.at[order[n], j], sibling).wait_recv()

    def partial_parts(t):
        for k in range(2):
            d = k + c * (3 - 2 * k)
            src = wv.at[pl.ds(k * ROWS, ROWS), pl.ds(pl.multiple_of(t * TILE, TILE), TILE)]
            to = device(zh, t % 2, y, (x + d) % 4, z)
            yield k, d, src, to, (d == 0) & (c == t % 2)

    def send_partials(t):
        for k, d, src, to, mine in partial_parts(t):
            @pl.when(mine)
            def _():
                pltpu.make_async_copy(src, got.at[t // 2, x], plocal.at[t // 2]).start()

            @pl.when(jnp.logical_not(mine))
            def _():
                remote(src, got.at[t // 2, x], psend.at[k, t], precv.at[t // 2, (4 - d) % 4], to).start()

    def compute(tokens, x_of, dy_of, first=False, last=False):
        for k in range(2):
            for h in range(2):
                wt = wv[pl.ds(k * ROWS, ROWS), pl.ds(h * HALF, HALF)]
                q = lax.dot_general(x_of(h, slice(None)), wt, (((1,), (1,)), ((), ())), preferred_element_type=jnp.float32)
                if h == 0:
                    pre[k, pl.ds(0, tokens)] = q
                else:
                    pre[k, pl.ds(0, tokens)] += q
        for k in range(2):
            hid = dy_of(k).astype(jnp.float32) * slope(pre[k, pl.ds(0, tokens)])
            ht[pl.ds(k * ROWS, ROWS), pl.ds(0, tokens)] = hid.T.astype(jnp.bfloat16)
        for h in range(2):
            @pl.loop(0, HALF // WIDE)
            def _(t):
                cols = pl.ds(pl.multiple_of(t * WIDE, WIDE), WIDE)
                wide = pl.ds(pl.multiple_of(h * HALF + t * WIDE, WIDE), WIDE)
                g = jnp.dot(ht[:, pl.ds(0, tokens)], x_of(h, cols), preferred_element_type=jnp.float32)
                if not first:
                    g = g + acc[:, wide]
                if not last:
                    acc[:, wide] = g
                else:
                    wv[:, wide] = g.astype(jnp.bfloat16)
                    for j in range(WIDE // TILE):
                        send_partials((h * HALF // WIDE + t) * (WIDE // TILE) + j)

    def compute_soon(zz, first=False, last=False):
        def x_of(h, cols):
            part = xs[h, zz, :, pl.ds(0, SOON), cols]
            return part.reshape(4 * SOON, part.shape[-1])

        def dy_of(k):
            return dv[k, zz, :, pl.ds(0, SOON), :].reshape(4 * SOON, ROWS)

        compute(4 * SOON, x_of, dy_of, first, last)

    def compute_late():
        def x_of(h, cols):
            part = xs[h, :, :, pl.ds(SOON, LATE), cols]
            return part.reshape(16 * LATE, part.shape[-1])

        def dy_of(k):
            return dv[k, :, :, pl.ds(SOON, LATE), :].reshape(16 * LATE, ROWS)

        compute(16 * LATE, x_of, dy_of)

    power = e_ref[...].astype(jnp.float32).T
    bigger, smaller = jnp.exp2(power), jnp.exp2(-power)
    for b in range(D // 128):
        cols = pl.ds(b * 128, 128)
        up[:, cols] = jnp.broadcast_to(bigger[:, b:b + 1], (ROWS, 128)).astype(jnp.bfloat16)
        down[:, cols] = jnp.broadcast_to(smaller[:, b:b + 1], (ROWS, 128)).astype(jnp.bfloat16)

    for j in range(2):
        late_y(2 + j).wait_recv()

    late_share(0)
    for n in range(1, 4):
        make_dy(order[n])
    from_z(1)
    forward(0)
    from_z(2)
    forward_w()
    send_dy(order[0])
    send_dy(order[1])
    forward(1)
    from_z(3)

    @pl.when(z < 3)
    def _():
        late_z(0, z, at_z(z + 1)).start()

    @pl.when(z > 0)
    def _():
        late_z(1, z, at_z(z - 1)).start()

    from_far(0)
    forward(2)
    late_from_z(1)
    wait_w()
    wait_dy(order[0])
    send_dy(order[2])
    send_dy(order[3])
    from_sibling(0)
    compute_soon(order[0], first=True)
    late_from_z(2)
    from_far(1)
    wait_dy(order[1])
    from_sibling(1)
    compute_soon(order[1])
    forward(3)
    late_from_z(3)
    from_far(2)
    wait_dy(order[2])
    from_sibling(2)
    compute_soon(order[2])
    wait_dy(order[3])
    for k in range(4):
        remote(late_block(0), late_block(0), lcsend.at[0], lcrecv.at[k], sibling).wait_recv()
    compute_late()
    from_far(3)
    from_sibling(3)
    w_forward().wait_send()
    compute_soon(order[3], last=True)
    piece = wv.at[pl.ds(0, ROWS), pl.ds(0, TILE)]
    owned = got.at[0, 0]
    crossing = []
    for i in range(TILES // 2):
        t = 2 * i + c
        cols = pl.ds(pl.multiple_of(t * TILE, TILE), TILE)
        for q in range(1, 4):
            remote(piece, owned, psend.at[0, 0], precv.at[i, q], sibling).wait_recv()

        @pl.when(c == 0)
        def _():
            pltpu.make_async_copy(piece, owned, plocal.at[i]).wait()

        @pl.when(c == 1)
        def _():
            remote(piece, owned, psend.at[0, 0], precv.at[i, 0], sibling).wait_recv()

        shrink = down[:, cols].astype(jnp.float32)

        def coded(g):
            total = got[i, 2 * g].astype(jnp.float32) + got[i, 2 * g + 1].astype(jnp.float32)
            return jnp.clip(inner_rate * (total * shrink), -code_limit, code_limit).astype(jnp.bfloat16).astype(jnp.float32)

        terms[t, zh] = (coded(0) + coded(1)).astype(jnp.bfloat16)
        here = terms.at[t, zh]
        over = remote(here, here, fsend.at[i], frecv.at[i], other_half)
        beside = remote(here, here, bsend.at[i, 0], brecv.at[i, 0], sibling)
        over.start()
        beside.start()
        crossing += [over, beside]
    for load in loads:
        load.wait()

    def finish(t, slot):
        cols = pl.ds(pl.multiple_of(t * TILE, TILE), TILE)
        total = terms[t, 0].astype(jnp.float32) + terms[t, 1].astype(jnp.float32)
        decoded = total * up[:, cols].astype(jnp.float32) / 4.0
        new_moment = momentum_coef * mom[:, cols] + decoded
        mom[:, cols] = new_moment
        rows_out[:, cols] = (rows_in[:, cols].astype(jnp.float32) - outer_rate * (decoded + momentum_coef * new_moment)).astype(jnp.bfloat16)
        writes = [pltpu.make_async_copy(mom.at[:, cols], nm_ref.at[:, cols], out.at[slot, 0]),
                  pltpu.make_async_copy(rows_out.at[:, cols], np_ref.at[:, cols], out.at[slot, 1])]
        for write in writes:
            write.start()
        return writes

    writes = []
    for i in range(TILES // 2):
        t, u = 2 * i + c, 2 * i + 1 - c
        remote(owned, owned, fsend.at[i], frecv.at[i], other_half).wait_recv()
        there = terms.at[t, 1 - zh]
        after = remote(there, there, bsend.at[i, 1], brecv.at[i, 1], sibling)
        after.start()
        crossing.append(after)
        writes += finish(t, 2 * i)
        for j in range(2):
            remote(owned, owned, bsend.at[i, j], brecv.at[i, j], sibling).wait_recv()
        writes += finish(u, 2 * i + 1)
    for k in range(4):
        for j in range(4):
            remote(own, own, csend.at[k, j], crecv.at[k, j], sibling).wait_send()
        for j, n in ((0, SOON), (1, SOON), (2, cut), (3, SOON - cut)):
            src = place(y, z, c, 0, n)
            remote(src, src, ysend.at[k, j], yrecv.at[k, j], sibling).wait_send()

    for j in range(4):
        late_y(j).wait_send()
        remote(late_block(0), late_block(0), lcsend.at[j], lcrecv.at[0], sibling).wait_send()

    @pl.when(z < 3)
    def _():
        remote(own, own, zsend.at[0], zrecv.at[z], at_z(z + 1)).wait_send()
        late_z(0, z, at_z(z + 1)).wait_send()

    @pl.when(z > 0)
    def _():
        remote(own, own, zsend.at[1], zrecv.at[z], at_z(z - 1)).wait_send()
        late_z(1, z, at_z(z - 1)).wait_send()

    @pl.when(inner)
    def _():
        for n in range(1, 4):
            remote(own, own, zsend.at[1 + n], zrecv.at[0], sibling).wait_send()
            late_z(1 + n, order[n], sibling).wait_send()

    for s in near:
        s.wait_send()
    for n in range(4):
        for src, slot_to, to, k, mine in dy_parts(order[n]):
            @pl.when(jnp.logical_not(mine))
            def _():
                remote(src, dv.at[0, 0], dsend.at[k, order[n]], drecv.at[0, 0], sibling).wait_send()

    for s in crossing:
        s.wait_send()
    for t in range(TILES):
        for k, d, src, to, mine in partial_parts(t):
            @pl.when(jnp.logical_not(mine))
            def _():
                remote(src, owned, psend.at[k, t], precv.at[0, 0], sibling).wait_send()
    for write in writes:
        write.wait()


DMA = pltpu.SemaphoreType.DMA


def per_device(features, cotangent, up_rows, moment, exponents):
    bf16 = jnp.bfloat16
    f32 = jnp.float32
    return pl.pallas_call(
        work_kernel,
        out_shape=[jax.ShapeDtypeStruct((ROWS, D), bf16), jax.ShapeDtypeStruct((ROWS, D), f32)],
        in_specs=[ANY] * 4 + [pl.BlockSpec(memory_space=pltpu.VMEM)], out_specs=[ANY] * 2,
        scratch_shapes=[
            pltpu.VMEM((2, 4, 4, SEED, HALF), bf16), pltpu.VMEM((2, TOK, HALF), bf16), pltpu.VMEM((2 * ROWS, D), bf16),
            pltpu.VMEM((2, 4, 4, SEED, ROWS), bf16), pltpu.VMEM((2 * ROWS, D), f32),
            pltpu.VMEM((2, 4 * SOON, ROWS), f32), pltpu.VMEM((2 * ROWS, 4 * SOON), bf16),
            pltpu.VMEM((TILES // 2, 4, ROWS, TILE), bf16), pltpu.VMEM((TILES, 2, ROWS, TILE), bf16),
            pltpu.VMEM((ROWS, D), f32), pltpu.VMEM((ROWS, D), bf16), pltpu.VMEM((ROWS, D), bf16),
            pltpu.VMEM((ROWS, D), bf16), pltpu.VMEM((ROWS, D), bf16),
            pltpu.VMEM((ROWS, TOKENS), bf16), pltpu.VMEM((TOKENS, ROWS), f32), pltpu.VMEM((2, 4, 4, SEED, ROWS), bf16),
            DMA((2,)), DMA((2,)), DMA((5,)), DMA((4,)), DMA((4, 4)), DMA((4, 4)), DMA((4, 4)), DMA((4, 4)),
            DMA((4,)), DMA((4,)), DMA((5,)), DMA((4,)), DMA((4,)), DMA((4,)),
            DMA((3,)), DMA((2, 2)), DMA((2, 4)), DMA((2, 4)), DMA((4,)), DMA((7,)),
            DMA((2, TILES)), DMA((TILES // 2, 4)), DMA((TILES // 2,)), DMA((TILES // 2,)), DMA((TILES // 2,)),
            DMA((TILES // 2, 2)), DMA((TILES // 2, 2)), DMA((TILES, 2))],
        compiler_params=pltpu.CompilerParams(collective_id=0, has_side_effects=True, vmem_limit_bytes=60 * 2**20), name="work",
    )(features, up_rows, cotangent.T, moment, exponents.T)


def solution(mesh):
    return jax.shard_map(
        per_device,
        mesh=mesh,
        in_specs=(P(("rep", "fsdp"), None), P("rep", "fsdp"), P("fsdp", None), P("fsdp", None), P("fsdp", None)),
        out_specs=(P("fsdp", None), P("fsdp", None)),
        check_vma=False,
    )
```

```python
import functools

import jax
import jax.numpy as jnp
from jax import lax
from jax.experimental import pallas as pl
from jax.experimental.pallas import tpu as pltpu
from jax.sharding import PartitionSpec as P

inner_rate = 0.02
outer_rate = 0.7
momentum_coef = 0.9
code_limit = 448.0

D = 4096
HALF = D // 2
TOK = 56
SEED = 2 * TOK
LATE = 16
SOON = SEED - LATE
EARLY = 48
WIDE = 1024
TOKENS = 3584
ROWS = 224
HROWS = ROWS // 2
TILE = 256
TILES = D // TILE
MESH = pl.DeviceIdType.MESH
ANY = pl.BlockSpec(memory_space=pl.ANY)


def where_am_i():
    rep, at = lax.axis_index("rep"), lax.axis_index("fsdp")
    return rep // 2, rep % 2, at // 16, (at // 4) % 4, at % 4


def device(zh, c, y, x, z):
    return (zh * 2 + c, (y * 4 + x) * 4 + z)


def barrier(peers):
    sem = pltpu.get_barrier_semaphore()
    for peer in peers:
        pl.semaphore_signal(sem, inc=1, device_id=peer, device_id_type=MESH)
    pl.semaphore_wait(sem, len(peers))


def remote(src, dst, send_sem, recv_sem, peer):
    return pltpu.make_async_remote_copy(src, dst, send_sem, recv_sem, device_id=peer, device_id_type=MESH)


def slope(p):
    s = jax.nn.sigmoid(p)
    return s * (1.0 + p * (1.0 - s))


def work_kernel(f_ref, w_ref, d_ref, m_ref, e_ref, np_ref, nm_ref,
                xs, seed, wv, dv, acc, pre, ht, got, terms, mom, rows_in, rows_out, up, down, dt, turned, dn,
                seed_send, seed_recv, zsend, zrecv, ysend, yrecv, csend, crecv, lysend, lyrecv, lzsend, lzrecv, lcsend, lcrecv, wsend, wrecv, dsend, drecv, dlocal, local,
                psend, precv, plocal, fsend, frecv, bsend, brecv, out):
    zh, c, y, x, z = where_am_i()
    role = 1 - c

    def at_y(k):
        return device(zh, c, (y + k) % 4, x, z)

    sibling = device(zh, 1 - c, y, x, z)
    peers = [sibling, at_y(1), at_y(3)]
    peers += [device(zh, c, y, x, (z + k) % 4) for k in range(1, 4)]
    peers += [device(zh, k, y, (x + q) % 4, z) for q in range(1, 4) for k in range(2)]
    keep_w = pltpu.make_async_copy(w_ref, wv.at[pl.ds(0, ROWS)], local.at[1])

    load_d = pltpu.make_async_copy(d_ref, dt, local.at[0])
    load_d.start()

    @pl.when(role == 0)
    def _():
        keep_w.start()

    other_half = device(1 - zh, c, y, x, z)
    barrier(peers + [other_half])
    loads = [pltpu.make_async_copy(m_ref, mom, local.at[4]), pltpu.make_async_copy(w_ref, rows_in, local.at[5])]
    for load in loads:
        load.start()

    mirror = 3 - x
    owner = c == x // 2
    whole = f_ref.at[:, pl.ds(0, HALF)]

    def half(k):
        return f_ref.at[:, pl.ds(pl.multiple_of(k * HALF, HALF), HALF)]

    keep = pltpu.make_async_copy(half(c), seed.at[0], local.at[6])
    give = remote(half(1 - c), seed.at[0], seed_send.at[0], seed_recv.at[0], sibling)
    across = [remote(half(k), seed.at[1], seed_send.at[k], seed_recv.at[1], device(zh, k, y, mirror, z)) for k in range(2)]

    @pl.when(owner)
    def _():
        keep.start()
        give.start()

    @pl.when(jnp.logical_not(owner))
    def _():
        for s in across:
            s.start()

    near = []
    for k in range(2):
        src = w_ref.at[pl.ds(pl.multiple_of(c * HROWS, 16), HROWS)]
        dst = wv.at[pl.ds(pl.multiple_of((1 - k) * ROWS + c * HROWS, 16), HROWS)]
        near.append(remote(src, dst, wsend.at[k], wrecv.at[1 - k, c], device(zh, 1 - k, y, (x + 3 + 2 * k) % 4, z)))

    for k in range(2):
        @pl.when(x % 2 != k)
        def _():
            near[k].start()

    def place(yy, zz, core, lo=0, n=SOON):
        return xs.at[core, zz, yy, pl.ds(lo, n)]

    own = place(y, z, c)

    inner = (z == 1) | (z == 2)
    order = [z, z + 1 - 2 * (z % 2), jnp.where(z < 2, 2, 1), jnp.where(z < 2, 3, 0)]

    def at_z(zz):
        return device(zh, c, y, x, zz)

    def send_own(lo, n):
        src = place(y, z, c, lo, n)

        @pl.when(z < 3)
        def _():
            remote(src, src, zsend.at[0], zrecv.at[z], at_z(z + 1)).start()

        @pl.when(z > 0)
        def _():
            remote(src, src, zsend.at[1], zrecv.at[z], at_z(z - 1)).start()

        pass_on(0, lo, n)

    def pass_on(n, lo=0, rows=SOON):
        zz = order[n]
        src = place(y, zz, c, lo, rows)
        remote(src, src, ysend.at[n, 0], yrecv.at[zz, 0], at_y(1)).start()
        remote(src, src, ysend.at[n, 1], yrecv.at[zz, 1], at_y(3)).start()
        remote(src, src, csend.at[n, 0], crecv.at[zz, 0], sibling).start()

    @pl.when(owner)
    def _():
        keep.wait()

    @pl.when(jnp.logical_not(owner))
    def _():
        remote(whole, seed.at[0], seed_send.at[0], seed_recv.at[0], sibling).wait_recv()

    xs[c, z, y, pl.ds(0, EARLY)] = seed[0, pl.ds(0, EARLY)]
    send_own(0, EARLY)

    load_d.wait()
    for b in range(TOKENS // 256):
        turned[pl.ds(b * 256, 256), :] = dt[:, pl.ds(b * 256, 256)].astype(jnp.float32).T
    remote(whole, seed.at[1], seed_send.at[0], seed_recv.at[1], sibling).wait_recv()
    joined = jnp.concatenate([seed[0].astype(jnp.float32), seed[1].astype(jnp.float32)], axis=0)
    xs[c, z, y, pl.ds(EARLY, SEED - EARLY)] = joined[EARLY:].astype(jnp.bfloat16)
    send_own(EARLY, SOON - EARLY)

    def from_z(n):
        src = place(y, order[n], c)
        remote(src, src, zsend.at[1 + n], zrecv.at[order[n]], sibling).wait_recv()

        @pl.when(inner)
        def _():
            to = 3 - z if n == 1 else jnp.where(z == 1, 0, 3)
            remote(src, src, zsend.at[1 + n], zrecv.at[order[n]], at_z(to)).start()

        pass_on(n)

    def late(yy, k=None):
        if k is None:
            return xs.at[c, z, yy, pl.ds(SOON, LATE)]
        return xs.at[c, z, yy, pl.ds(SOON, LATE), pl.ds(k * (HALF // 2), HALF // 2)]

    def late_y(j):
        src = [late(y), late(y), late((y + 3) % 4, 0), late((y + 1) % 4, 1)][j]
        return remote(src, src, lysend.at[j], lyrecv.at[j], at_y(1 if j % 2 == 0 else 3))

    def late_block(zz):
        return xs.at[c, zz, :, pl.ds(SOON, LATE)]

    def late_z(k, zz, to):
        return remote(late_block(zz), late_block(zz), lzsend.at[k], lzrecv.at[zz], to)

    def late_share(n):
        src = late_block(order[n])
        remote(src, src, lcsend.at[n], lcrecv.at[order[n]], sibling).start()

    def late_from_z(n):
        late_z(1 + n, order[n], sibling).wait_recv()

        @pl.when(inner)
        def _():
            late_z(1 + n, order[n], at_z(3 - z if n == 1 else jnp.where(z == 1, 0, 3))).start()

        late_share(n)

    late_y(0).start()
    late_y(1).start()

    def w_forward():
        row = (1 - role) * HROWS
        src = wv.at[pl.ds(pl.multiple_of((1 - role) * ROWS + row, 16), HROWS)]
        dst = wv.at[pl.ds(pl.multiple_of(ROWS + row, 16), HROWS)]
        return remote(src, dst, wsend.at[2], wrecv.at[1, 1 - role], device(zh, 0, y, (x + 3 + 2 * role) % 4, z))

    def forward_w():
        remote(w_ref.at[pl.ds(0, HROWS)], wv.at[pl.ds(0, HROWS)], wsend.at[2], wrecv.at[1 - role, 1 - role], sibling).wait_recv()
        w_forward().start()

    def wait_w():
        def arrived(k, j):
            remote(w_ref.at[pl.ds(0, HROWS)], wv.at[pl.ds(0, HROWS)], wsend.at[2], wrecv.at[k, j], sibling).wait_recv()

        arrived(1 - role, role)

        @pl.when(role == 0)
        def _():
            keep_w.wait()

        @pl.when(role == 1)
        def _():
            arrived(1, 0)
            arrived(1, 1)

    def make_dy(zz):
        for h, pair in enumerate(((0, 3), (1, 2))):
            for yy in range(4):
                pair_of = [jnp.where(c == 0, pair[0], pair[1]), jnp.where(c == 0, pair[1], pair[0])]
                both = [turned[pl.ds(pl.multiple_of(((yy * 4 + at) * 4 + zz) * TOK, 8), TOK), :] for at in pair_of]
                dn[h, zz, yy] = jnp.concatenate(both, axis=0).astype(jnp.bfloat16)

    def dy_parts(zz):
        for k in range(2):
            to = 2 * c + k
            d = (x - to + 4) % 4
            h = jnp.where((to == 0) | (to == 3), 0, 1)
            yield dn.at[h, zz], (d + d // 2) % 2, device(zh, 1 - d // 2, y, to, z), k, (d == 0) & (c == 1)

    def send_dy(zz):
        for src, slot_to, to, k, mine in dy_parts(zz):
            @pl.when(mine)
            def _():
                pltpu.make_async_copy(src, dv.at[0, zz], dlocal.at[zz]).start()

            @pl.when(jnp.logical_not(mine))
            def _():
                remote(src, dv.at[slot_to, zz], dsend.at[k, zz], drecv.at[slot_to, zz], to).start()

    def wait_dy(zz):
        here = (c == 1) & (x // 2 == 1)

        @pl.when(here)
        def _():
            pltpu.make_async_copy(dn.at[0, zz], dv.at[0, zz], dlocal.at[zz]).wait()

        @pl.when(jnp.logical_not(here))
        def _():
            remote(dn.at[0, zz], dv.at[0, zz], dsend.at[0, zz], drecv.at[0, zz], sibling).wait_recv()

        remote(dn.at[0, zz], dv.at[1, zz], dsend.at[0, zz], drecv.at[1, zz], sibling).wait_recv()

    for k in range(2):
        @pl.when(x % 2 == k)
        def _():
            near[k].start()

    make_dy(order[0])
    for j in range(2):
        late_y(j).wait_recv()
        late_y(2 + j).start()

    cut = SOON // 2

    def forward(n):
        zz = order[n]
        above, below = (y + 3) % 4, (y + 1) % 4
        remote(own, place(above, zz, c), ysend.at[n, 0], yrecv.at[zz, 0], at_y(1)).wait_recv()
        src = place(above, zz, c, 0, cut)
        remote(src, src, ysend.at[n, 2], yrecv.at[zz, 2], at_y(1)).start()
        src = place(above, zz, c)
        remote(src, src, csend.at[n, 1], crecv.at[zz, 1], sibling).start()
        remote(own, place(below, zz, c), ysend.at[n, 1], yrecv.at[zz, 1], at_y(3)).wait_recv()
        src = place(below, zz, c, cut, SOON - cut)
        remote(src, src, ysend.at[n, 3], yrecv.at[zz, 3], at_y(3)).start()
        src = place(below, zz, c)
        remote(src, src, csend.at[n, 2], crecv.at[zz, 2], sibling).start()

    def from_far(n):
        zz, far = order[n], (y + 2) % 4
        src = place(far, zz, c, 0, cut)
        remote(src, src, ysend.at[n, 2], yrecv.at[zz, 2], at_y(1)).wait_recv()
        src = place(far, zz, c, cut, SOON - cut)
        remote(src, src, ysend.at[n, 3], yrecv.at[zz, 3], at_y(3)).wait_recv()
        src = place(far, zz, c)
        remote(src, src, csend.at[n, 3], crecv.at[zz, 3], sibling).start()

    def from_sibling(n):
        for j in range(4):
            remote(own, own, csend.at[n, j], crecv.at[order[n], j], sibling).wait_recv()

    def partial_parts(t):
        for k in range(2):
            d = k + role * (3 - 2 * k)
            src = wv.at[pl.ds(k * ROWS, ROWS), pl.ds(pl.multiple_of(t * TILE, TILE), TILE)]
            to = device(zh, t % 2, y, (x + d) % 4, z)
            yield k, d, src, to, (d == 0) & (c == t % 2)

    def send_partials(t):
        for k, d, src, to, mine in partial_parts(t):
            @pl.when(mine)
            def _():
                pltpu.make_async_copy(src, got.at[t // 2, x], plocal.at[t // 2]).start()

            @pl.when(jnp.logical_not(mine))
            def _():
                remote(src, got.at[t // 2, x], psend.at[k, t], precv.at[t // 2, (4 - d) % 4], to).start()

    def compute(soon=(), late=False, first=False, last=False):
        tokens = 4 * SOON * len(soon) + 16 * LATE * late

        def x_of(h, cols):
            parts = [xs[h, order[n], :, pl.ds(0, SOON), cols] for n in soon]
            if late:
                parts.append(xs[h, :, :, pl.ds(SOON, LATE), cols])
            return jnp.concatenate([p.reshape(-1, p.shape[-1]) for p in parts], axis=0)

        def dy_of(k):
            parts = [dv[k, order[n], :, pl.ds(0, SOON), :] for n in soon]
            if late:
                parts.append(dv[k, :, :, pl.ds(SOON, LATE), :])
            return jnp.concatenate([p.reshape(-1, ROWS) for p in parts], axis=0)

        for k in range(2):
            for h in range(2):
                wt = wv[pl.ds(k * ROWS, ROWS), pl.ds(h * HALF, HALF)]
                q = lax.dot_general(x_of(h, slice(None)), wt, (((1,), (1,)), ((), ())), preferred_element_type=jnp.float32)
                if h == 0:
                    pre[k, pl.ds(0, tokens)] = q
                else:
                    pre[k, pl.ds(0, tokens)] += q
        for k in range(2):
            hid = dy_of(k).astype(jnp.float32) * slope(pre[k, pl.ds(0, tokens)])
            ht[pl.ds(k * ROWS, ROWS), pl.ds(0, tokens)] = hid.T.astype(jnp.bfloat16)
        for h in range(2):
            @pl.loop(0, HALF // WIDE)
            def _(t):
                cols = pl.ds(pl.multiple_of(t * WIDE, WIDE), WIDE)
                wide = pl.ds(pl.multiple_of(h * HALF + t * WIDE, WIDE), WIDE)
                g = jnp.dot(ht[:, pl.ds(0, tokens)], x_of(h, cols), preferred_element_type=jnp.float32)
                if not first:
                    g = g + acc[:, wide]
                if not last:
                    acc[:, wide] = g
                else:
                    wv[:, wide] = g.astype(jnp.bfloat16)
                    for j in range(WIDE // TILE):
                        send_partials((h * HALF // WIDE + t) * (WIDE // TILE) + j)

    power = e_ref[...].astype(jnp.float32).T
    bigger, smaller = jnp.exp2(power), jnp.exp2(-power)
    for b in range(D // 128):
        cols = pl.ds(b * 128, 128)
        up[:, cols] = jnp.broadcast_to(bigger[:, b:b + 1], (ROWS, 128)).astype(jnp.bfloat16)
        down[:, cols] = jnp.broadcast_to(smaller[:, b:b + 1], (ROWS, 128)).astype(jnp.bfloat16)

    for j in range(2):
        late_y(2 + j).wait_recv()

    late_share(0)
    for n in range(1, 4):
        make_dy(order[n])
    from_z(1)
    forward(0)
    from_z(2)
    forward_w()
    send_dy(order[0])
    send_dy(order[1])
    forward(1)
    from_z(3)
    @pl.when(z < 3)
    def _():
        late_z(0, z, at_z(z + 1)).start()

    @pl.when(z > 0)
    def _():
        late_z(1, z, at_z(z - 1)).start()

    from_far(0)
    forward(2)
    late_from_z(1)
    wait_w()
    wait_dy(order[0])
    send_dy(order[2])
    send_dy(order[3])
    from_sibling(0)
    late_from_z(2)
    from_far(1)
    wait_dy(order[1])
    from_sibling(1)
    compute((0, 1), first=True)
    forward(3)
    late_from_z(3)
    from_far(2)
    wait_dy(order[2])
    from_sibling(2)
    wait_dy(order[3])
    for k in range(4):
        remote(late_block(0), late_block(0), lcsend.at[0], lcrecv.at[k], sibling).wait_recv()
    compute((2,), late=True)
    from_far(3)
    from_sibling(3)
    w_forward().wait_send()
    compute((3,), last=True)
    piece = wv.at[pl.ds(0, ROWS), pl.ds(0, TILE)]
    owned = got.at[0, 0]
    crossing = []
    for i in range(TILES // 2):
        t = 2 * i + c
        cols = pl.ds(pl.multiple_of(t * TILE, TILE), TILE)
        for q in range(1, 4):
            remote(piece, owned, psend.at[0, 0], precv.at[i, q], sibling).wait_recv()

        @pl.when(c == 1)
        def _():
            pltpu.make_async_copy(piece, owned, plocal.at[i]).wait()

        @pl.when(c == 0)
        def _():
            remote(piece, owned, psend.at[0, 0], precv.at[i, 0], sibling).wait_recv()

        shrink = down[:, cols].astype(jnp.float32)

        def coded(g):
            total = got[i, 2 * g].astype(jnp.float32) + got[i, 2 * g + 1].astype(jnp.float32)
            return jnp.clip(inner_rate * (total * shrink), -code_limit, code_limit).astype(jnp.bfloat16).astype(jnp.float32)

        terms[t, zh] = (coded(0) + coded(1)).astype(jnp.bfloat16)
        here = terms.at[t, zh]
        over = remote(here, here, fsend.at[i], frecv.at[i], other_half)
        beside = remote(here, here, bsend.at[i, 0], brecv.at[i, 0], sibling)
        over.start()
        beside.start()
        crossing += [over, beside]
    for load in loads:
        load.wait()

    def finish(t, slot):
        cols = pl.ds(pl.multiple_of(t * TILE, TILE), TILE)
        total = terms[t, 0].astype(jnp.float32) + terms[t, 1].astype(jnp.float32)
        decoded = total * up[:, cols].astype(jnp.float32) / 4.0
        new_moment = momentum_coef * mom[:, cols] + decoded
        mom[:, cols] = new_moment
        rows_out[:, cols] = (rows_in[:, cols].astype(jnp.float32) - outer_rate * (decoded + momentum_coef * new_moment)).astype(jnp.bfloat16)
        writes = [pltpu.make_async_copy(mom.at[:, cols], nm_ref.at[:, cols], out.at[slot, 0]),
                  pltpu.make_async_copy(rows_out.at[:, cols], np_ref.at[:, cols], out.at[slot, 1])]
        for write in writes:
            write.start()
        return writes

    writes = []
    for i in range(TILES // 2):
        t, u = 2 * i + c, 2 * i + 1 - c
        remote(owned, owned, fsend.at[i], frecv.at[i], other_half).wait_recv()
        there = terms.at[t, 1 - zh]
        after = remote(there, there, bsend.at[i, 1], brecv.at[i, 1], sibling)
        after.start()
        crossing.append(after)
        writes += finish(t, 2 * i)
        for j in range(2):
            remote(owned, owned, bsend.at[i, j], brecv.at[i, j], sibling).wait_recv()
        writes += finish(u, 2 * i + 1)
    @pl.when(owner)
    def _():
        give.wait_send()

    @pl.when(jnp.logical_not(owner))
    def _():
        for s in across:
            s.wait_send()

    for k in range(4):
        for j in range(4):
            remote(own, own, csend.at[k, j], crecv.at[k, j], sibling).wait_send()
        for j, n in ((0, SOON), (1, SOON), (2, cut), (3, SOON - cut)):
            src = place(y, z, c, 0, n)
            remote(src, src, ysend.at[k, j], yrecv.at[k, j], sibling).wait_send()

    for j in range(4):
        late_y(j).wait_send()
        remote(late_block(0), late_block(0), lcsend.at[j], lcrecv.at[0], sibling).wait_send()

    @pl.when(z < 3)
    def _():
        remote(own, own, zsend.at[0], zrecv.at[z], at_z(z + 1)).wait_send()
        late_z(0, z, at_z(z + 1)).wait_send()

    @pl.when(z > 0)
    def _():
        remote(own, own, zsend.at[1], zrecv.at[z], at_z(z - 1)).wait_send()
        late_z(1, z, at_z(z - 1)).wait_send()

    @pl.when(inner)
    def _():
        for n in range(1, 4):
            remote(own, own, zsend.at[1 + n], zrecv.at[0], sibling).wait_send()
            late_z(1 + n, order[n], sibling).wait_send()

    for s in near:
        s.wait_send()
    for n in range(4):
        for src, slot_to, to, k, mine in dy_parts(order[n]):
            @pl.when(jnp.logical_not(mine))
            def _():
                remote(src, dv.at[0, 0], dsend.at[k, order[n]], drecv.at[0, 0], sibling).wait_send()

    for s in crossing:
        s.wait_send()
    for t in range(TILES):
        for k, d, src, to, mine in partial_parts(t):
            @pl.when(jnp.logical_not(mine))
            def _():
                remote(src, owned, psend.at[k, t], precv.at[0, 0], sibling).wait_send()
    for write in writes:
        write.wait()


DMA = pltpu.SemaphoreType.DMA


def per_device(features, cotangent, up_rows, moment, exponents):
    bf16 = jnp.bfloat16
    f32 = jnp.float32
    return pl.pallas_call(
        work_kernel,
        out_shape=[jax.ShapeDtypeStruct((ROWS, D), bf16), jax.ShapeDtypeStruct((ROWS, D), f32)],
        in_specs=[ANY] * 4 + [pl.BlockSpec(memory_space=pltpu.VMEM)], out_specs=[ANY] * 2,
        scratch_shapes=[
            pltpu.VMEM((2, 4, 4, SEED, HALF), bf16), pltpu.VMEM((2, TOK, HALF), bf16), pltpu.VMEM((2 * ROWS, D), bf16),
            pltpu.VMEM((2, 4, 4, SEED, ROWS), bf16), pltpu.VMEM((2 * ROWS, D), f32),
            pltpu.VMEM((2, 8 * SOON, ROWS), f32), pltpu.VMEM((2 * ROWS, 8 * SOON), bf16),
            pltpu.VMEM((TILES // 2, 4, ROWS, TILE), bf16), pltpu.VMEM((TILES, 2, ROWS, TILE), bf16),
            pltpu.VMEM((ROWS, D), f32), pltpu.VMEM((ROWS, D), bf16), pltpu.VMEM((ROWS, D), bf16),
            pltpu.VMEM((ROWS, D), bf16), pltpu.VMEM((ROWS, D), bf16),
            pltpu.VMEM((ROWS, TOKENS), bf16), pltpu.VMEM((TOKENS, ROWS), f32), pltpu.VMEM((2, 4, 4, SEED, ROWS), bf16),
            DMA((2,)), DMA((2,)), DMA((5,)), DMA((4,)), DMA((4, 4)), DMA((4, 4)), DMA((4, 4)), DMA((4, 4)),
            DMA((4,)), DMA((4,)), DMA((5,)), DMA((4,)), DMA((4,)), DMA((4,)),
            DMA((3,)), DMA((2, 2)), DMA((2, 4)), DMA((2, 4)), DMA((4,)), DMA((7,)),
            DMA((2, TILES)), DMA((TILES // 2, 4)), DMA((TILES // 2,)), DMA((TILES // 2,)), DMA((TILES // 2,)),
            DMA((TILES // 2, 2)), DMA((TILES // 2, 2)), DMA((TILES, 2))],
        compiler_params=pltpu.CompilerParams(collective_id=0, has_side_effects=True, vmem_limit_bytes=60 * 2**20), name="work",
    )(features, up_rows, cotangent.T, moment, exponents.T)


def solution(mesh):
    return jax.shard_map(
        per_device,
        mesh=mesh,
        in_specs=(P(("rep", "fsdp"), None), P("rep", "fsdp"), P("fsdp", None), P("fsdp", None), P("fsdp", None)),
        out_specs=(P("fsdp", None), P("fsdp", None)),
        check_vma=False,
    )
```

```python
import functools

import jax
import jax.numpy as jnp
from jax import lax
from jax.experimental import pallas as pl
from jax.experimental.pallas import tpu as pltpu
from jax.sharding import PartitionSpec as P

inner_rate = 0.02
outer_rate = 0.7
momentum_coef = 0.9
code_limit = 448.0

D = 4096
HALF = D // 2
TOK = 56
SEED = 2 * TOK
LATE = 16
SOON = SEED - LATE
EARLY = 48
WIDE = 1024
TOKENS = 3584
ROWS = 224
HROWS = ROWS // 2
TILE = 256
TILES = D // TILE
LAG = 3
MESH = pl.DeviceIdType.MESH
ANY = pl.BlockSpec(memory_space=pl.ANY)


def where_am_i():
    rep, at = lax.axis_index("rep"), lax.axis_index("fsdp")
    return rep // 2, rep % 2, at // 16, (at // 4) % 4, at % 4


def device(zh, c, y, x, z):
    return (zh * 2 + c, (y * 4 + x) * 4 + z)


def barrier(peers):
    sem = pltpu.get_barrier_semaphore()
    for peer in peers:
        pl.semaphore_signal(sem, inc=1, device_id=peer, device_id_type=MESH)
    pl.semaphore_wait(sem, len(peers))


def remote(src, dst, send_sem, recv_sem, peer):
    return pltpu.make_async_remote_copy(src, dst, send_sem, recv_sem, device_id=peer, device_id_type=MESH)


def slope(p):
    s = jax.nn.sigmoid(p)
    return s * (1.0 + p * (1.0 - s))


def work_kernel(f_ref, w_ref, d_ref, m_ref, e_ref, np_ref, nm_ref,
                xs, seed, wv, dv, acc, pre, ht, got, terms, mom, rows_in, rows_out, up, down, dt, turned, dn,
                seed_send, seed_recv, zsend, zrecv, ysend, yrecv, csend, crecv, lysend, lyrecv, lzsend, lzrecv, lcsend, lcrecv, wsend, wrecv, dsend, drecv, dlocal, local,
                psend, precv, plocal, fsend, frecv, bsend, brecv, out):
    zh, c, y, x, z = where_am_i()
    role = 1 - c

    def at_y(k):
        return device(zh, c, (y + k) % 4, x, z)

    sibling = device(zh, 1 - c, y, x, z)
    peers = [sibling, at_y(1), at_y(3)]
    peers += [device(zh, c, y, x, (z + k) % 4) for k in range(1, 4)]
    peers += [device(zh, k, y, (x + q) % 4, z) for q in range(1, 4) for k in range(2)]
    keep_w = pltpu.make_async_copy(w_ref, wv.at[pl.ds(0, ROWS)], local.at[1])

    load_d = pltpu.make_async_copy(d_ref, dt, local.at[0])
    load_d.start()

    @pl.when(role == 0)
    def _():
        keep_w.start()

    other_half = device(1 - zh, c, y, x, z)
    barrier(peers + [other_half])
    loads = [pltpu.make_async_copy(m_ref, mom, local.at[4]), pltpu.make_async_copy(w_ref, rows_in, local.at[5])]
    for load in loads:
        load.start()

    mirror = 3 - x
    owner = c == x // 2
    whole = f_ref.at[:, pl.ds(0, HALF)]

    def half(k):
        return f_ref.at[:, pl.ds(pl.multiple_of(k * HALF, HALF), HALF)]

    keep = pltpu.make_async_copy(half(c), seed.at[0], local.at[6])
    give = remote(half(1 - c), seed.at[0], seed_send.at[0], seed_recv.at[0], sibling)
    across = [remote(half(k), seed.at[1], seed_send.at[k], seed_recv.at[1], device(zh, k, y, mirror, z)) for k in range(2)]

    @pl.when(owner)
    def _():
        keep.start()
        give.start()

    @pl.when(jnp.logical_not(owner))
    def _():
        for s in across:
            s.start()

    near = []
    for k in range(2):
        src = w_ref.at[pl.ds(pl.multiple_of(c * HROWS, 16), HROWS)]
        dst = wv.at[pl.ds(pl.multiple_of((1 - k) * ROWS + c * HROWS, 16), HROWS)]
        near.append(remote(src, dst, wsend.at[k], wrecv.at[1 - k, c], device(zh, 1 - k, y, (x + 3 + 2 * k) % 4, z)))

    for k in range(2):
        @pl.when(x % 2 != k)
        def _():
            near[k].start()

    def place(yy, zz, core, lo=0, n=SOON):
        return xs.at[core, zz, yy, pl.ds(lo, n)]

    own = place(y, z, c)

    inner = (z == 1) | (z == 2)
    order = [z, z + 1 - 2 * (z % 2), jnp.where(z < 2, 2, 1), jnp.where(z < 2, 3, 0)]

    def at_z(zz):
        return device(zh, c, y, x, zz)

    def send_own(lo, n):
        src = place(y, z, c, lo, n)

        @pl.when(z < 3)
        def _():
            remote(src, src, zsend.at[0], zrecv.at[z], at_z(z + 1)).start()

        @pl.when(z > 0)
        def _():
            remote(src, src, zsend.at[1], zrecv.at[z], at_z(z - 1)).start()

        pass_on(0, lo, n)

    def pass_on(n, lo=0, rows=SOON):
        zz = order[n]
        src = place(y, zz, c, lo, rows)
        remote(src, src, ysend.at[n, 0], yrecv.at[zz, 0], at_y(1)).start()
        remote(src, src, ysend.at[n, 1], yrecv.at[zz, 1], at_y(3)).start()
        remote(src, src, csend.at[n, 0], crecv.at[zz, 0], sibling).start()

    @pl.when(owner)
    def _():
        keep.wait()

    @pl.when(jnp.logical_not(owner))
    def _():
        remote(whole, seed.at[0], seed_send.at[0], seed_recv.at[0], sibling).wait_recv()

    xs[c, z, y, pl.ds(0, EARLY)] = seed[0, pl.ds(0, EARLY)]
    send_own(0, EARLY)

    load_d.wait()
    for b in range(TOKENS // 256):
        turned[pl.ds(b * 256, 256), :] = dt[:, pl.ds(b * 256, 256)].astype(jnp.float32).T
    remote(whole, seed.at[1], seed_send.at[0], seed_recv.at[1], sibling).wait_recv()
    joined = jnp.concatenate([seed[0].astype(jnp.float32), seed[1].astype(jnp.float32)], axis=0)
    xs[c, z, y, pl.ds(EARLY, SEED - EARLY)] = joined[EARLY:].astype(jnp.bfloat16)
    send_own(EARLY, SOON - EARLY)

    def from_z(n):
        src = place(y, order[n], c)
        remote(src, src, zsend.at[1 + n], zrecv.at[order[n]], sibling).wait_recv()

        @pl.when(inner)
        def _():
            to = 3 - z if n == 1 else jnp.where(z == 1, 0, 3)
            remote(src, src, zsend.at[1 + n], zrecv.at[order[n]], at_z(to)).start()

        pass_on(n)

    def late(yy, k=None):
        if k is None:
            return xs.at[c, z, yy, pl.ds(SOON, LATE)]
        return xs.at[c, z, yy, pl.ds(SOON, LATE), pl.ds(k * (HALF // 2), HALF // 2)]

    def late_y(j):
        src = [late(y), late(y), late((y + 3) % 4, 0), late((y + 1) % 4, 1)][j]
        return remote(src, src, lysend.at[j], lyrecv.at[j], at_y(1 if j % 2 == 0 else 3))

    def late_block(zz):
        return xs.at[c, zz, :, pl.ds(SOON, LATE)]

    def late_z(k, zz, to):
        return remote(late_block(zz), late_block(zz), lzsend.at[k], lzrecv.at[zz], to)

    def late_share(n):
        src = late_block(order[n])
        remote(src, src, lcsend.at[n], lcrecv.at[order[n]], sibling).start()

    def late_from_z(n):
        late_z(1 + n, order[n], sibling).wait_recv()

        @pl.when(inner)
        def _():
            late_z(1 + n, order[n], at_z(3 - z if n == 1 else jnp.where(z == 1, 0, 3))).start()

        late_share(n)

    late_y(0).start()
    late_y(1).start()

    def w_forward():
        row = (1 - role) * HROWS
        src = wv.at[pl.ds(pl.multiple_of((1 - role) * ROWS + row, 16), HROWS)]
        dst = wv.at[pl.ds(pl.multiple_of(ROWS + row, 16), HROWS)]
        return remote(src, dst, wsend.at[2], wrecv.at[1, 1 - role], device(zh, 0, y, (x + 3 + 2 * role) % 4, z))

    def forward_w():
        remote(w_ref.at[pl.ds(0, HROWS)], wv.at[pl.ds(0, HROWS)], wsend.at[2], wrecv.at[1 - role, 1 - role], sibling).wait_recv()
        w_forward().start()

    def wait_w():
        def arrived(k, j):
            remote(w_ref.at[pl.ds(0, HROWS)], wv.at[pl.ds(0, HROWS)], wsend.at[2], wrecv.at[k, j], sibling).wait_recv()

        arrived(1 - role, role)

        @pl.when(role == 0)
        def _():
            keep_w.wait()

        @pl.when(role == 1)
        def _():
            arrived(1, 0)
            arrived(1, 1)

    def make_dy(zz):
        for h, pair in enumerate(((0, 3), (1, 2))):
            for yy in range(4):
                pair_of = [jnp.where(c == 0, pair[0], pair[1]), jnp.where(c == 0, pair[1], pair[0])]
                both = [turned[pl.ds(pl.multiple_of(((yy * 4 + at) * 4 + zz) * TOK, 8), TOK), :] for at in pair_of]
                dn[h, zz, yy] = jnp.concatenate(both, axis=0).astype(jnp.bfloat16)

    def dy_parts(zz):
        for k in range(2):
            to = 2 * c + k
            d = (x - to + 4) % 4
            h = jnp.where((to == 0) | (to == 3), 0, 1)
            yield dn.at[h, zz], (d + d // 2) % 2, device(zh, 1 - d // 2, y, to, z), k, (d == 0) & (c == 1)

    def send_dy(zz):
        for src, slot_to, to, k, mine in dy_parts(zz):
            @pl.when(mine)
            def _():
                pltpu.make_async_copy(src, dv.at[0, zz], dlocal.at[zz]).start()

            @pl.when(jnp.logical_not(mine))
            def _():
                remote(src, dv.at[slot_to, zz], dsend.at[k, zz], drecv.at[slot_to, zz], to).start()

    def wait_dy(zz):
        here = (c == 1) & (x // 2 == 1)

        @pl.when(here)
        def _():
            pltpu.make_async_copy(dn.at[0, zz], dv.at[0, zz], dlocal.at[zz]).wait()

        @pl.when(jnp.logical_not(here))
        def _():
            remote(dn.at[0, zz], dv.at[0, zz], dsend.at[0, zz], drecv.at[0, zz], sibling).wait_recv()

        remote(dn.at[0, zz], dv.at[1, zz], dsend.at[0, zz], drecv.at[1, zz], sibling).wait_recv()

    for k in range(2):
        @pl.when(x % 2 == k)
        def _():
            near[k].start()

    make_dy(order[0])
    for j in range(2):
        late_y(j).wait_recv()
        late_y(2 + j).start()

    cut = SOON // 2

    def forward(n):
        zz = order[n]
        above, below = (y + 3) % 4, (y + 1) % 4
        remote(own, place(above, zz, c), ysend.at[n, 0], yrecv.at[zz, 0], at_y(1)).wait_recv()
        src = place(above, zz, c, 0, cut)
        remote(src, src, ysend.at[n, 2], yrecv.at[zz, 2], at_y(1)).start()
        src = place(above, zz, c)
        remote(src, src, csend.at[n, 1], crecv.at[zz, 1], sibling).start()
        remote(own, place(below, zz, c), ysend.at[n, 1], yrecv.at[zz, 1], at_y(3)).wait_recv()
        src = place(below, zz, c, cut, SOON - cut)
        remote(src, src, ysend.at[n, 3], yrecv.at[zz, 3], at_y(3)).start()
        src = place(below, zz, c)
        remote(src, src, csend.at[n, 2], crecv.at[zz, 2], sibling).start()

    def from_far(n):
        zz, far = order[n], (y + 2) % 4
        src = place(far, zz, c, 0, cut)
        remote(src, src, ysend.at[n, 2], yrecv.at[zz, 2], at_y(1)).wait_recv()
        src = place(far, zz, c, cut, SOON - cut)
        remote(src, src, ysend.at[n, 3], yrecv.at[zz, 3], at_y(3)).wait_recv()
        src = place(far, zz, c)
        remote(src, src, csend.at[n, 3], crecv.at[zz, 3], sibling).start()

    def from_sibling(n):
        for j in range(4):
            remote(own, own, csend.at[n, j], crecv.at[order[n], j], sibling).wait_recv()

    def partial_parts(t):
        for k in range(2):
            d = k + role * (3 - 2 * k)
            src = wv.at[pl.ds(k * ROWS, ROWS), pl.ds(pl.multiple_of(t * TILE, TILE), TILE)]
            to = device(zh, t % 2, y, (x + d) % 4, z)
            yield k, d, src, to, (d == 0) & (c == t % 2)

    def send_partials(t):
        for k, d, src, to, mine in partial_parts(t):
            @pl.when(mine)
            def _():
                pltpu.make_async_copy(src, got.at[t // 2, x], plocal.at[t // 2]).start()

            @pl.when(jnp.logical_not(mine))
            def _():
                remote(src, got.at[t // 2, x], psend.at[k, t], precv.at[t // 2, (4 - d) % 4], to).start()

    def compute(soon=(), late=False, first=False, last=False):
        tokens = 4 * SOON * len(soon) + 16 * LATE * late

        def x_of(h, cols):
            parts = [xs[h, order[n], :, pl.ds(0, SOON), cols] for n in soon]
            if late:
                parts.append(xs[h, :, :, pl.ds(SOON, LATE), cols])
            return jnp.concatenate([p.reshape(-1, p.shape[-1]) for p in parts], axis=0)

        def dy_of(k):
            parts = [dv[k, order[n], :, pl.ds(0, SOON), :] for n in soon]
            if late:
                parts.append(dv[k, :, :, pl.ds(SOON, LATE), :])
            return jnp.concatenate([p.reshape(-1, ROWS) for p in parts], axis=0)

        for k in range(2):
            for h in range(2):
                wt = wv[pl.ds(k * ROWS, ROWS), pl.ds(h * HALF, HALF)]
                q = lax.dot_general(x_of(h, slice(None)), wt, (((1,), (1,)), ((), ())), preferred_element_type=jnp.float32)
                if h == 0:
                    pre[k, pl.ds(0, tokens)] = q
                else:
                    pre[k, pl.ds(0, tokens)] += q
        for k in range(2):
            hid = dy_of(k).astype(jnp.float32) * slope(pre[k, pl.ds(0, tokens)])
            ht[pl.ds(k * ROWS, ROWS), pl.ds(0, tokens)] = hid.T.astype(jnp.bfloat16)
        for h in range(2):
            @pl.loop(0, HALF // WIDE)
            def _(t):
                cols = pl.ds(pl.multiple_of(t * WIDE, WIDE), WIDE)
                wide = pl.ds(pl.multiple_of(h * HALF + t * WIDE, WIDE), WIDE)
                g = jnp.dot(ht[:, pl.ds(0, tokens)], x_of(h, cols), preferred_element_type=jnp.float32)
                if not first:
                    g = g + acc[:, wide]
                if not last:
                    acc[:, wide] = g
                else:
                    wv[:, wide] = g.astype(jnp.bfloat16)
                    for j in range(WIDE // TILE):
                        send_partials((h * HALF // WIDE + t) * (WIDE // TILE) + j)

    power = e_ref[...].astype(jnp.float32).T
    bigger, smaller = jnp.exp2(power), jnp.exp2(-power)
    for b in range(D // 128):
        cols = pl.ds(b * 128, 128)
        up[:, cols] = jnp.broadcast_to(bigger[:, b:b + 1], (ROWS, 128)).astype(jnp.bfloat16)
        down[:, cols] = jnp.broadcast_to(smaller[:, b:b + 1], (ROWS, 128)).astype(jnp.bfloat16)

    for j in range(2):
        late_y(2 + j).wait_recv()

    late_share(0)
    for n in range(1, 4):
        make_dy(order[n])
    from_z(1)
    forward(0)
    from_z(2)
    forward_w()
    send_dy(order[0])
    send_dy(order[1])
    forward(1)
    from_z(3)
    @pl.when(z < 3)
    def _():
        late_z(0, z, at_z(z + 1)).start()

    @pl.when(z > 0)
    def _():
        late_z(1, z, at_z(z - 1)).start()

    from_far(0)
    forward(2)
    late_from_z(1)
    wait_w()
    wait_dy(order[0])
    send_dy(order[2])
    send_dy(order[3])
    from_sibling(0)
    late_from_z(2)
    from_far(1)
    wait_dy(order[1])
    from_sibling(1)
    compute((0, 1), first=True)
    forward(3)
    late_from_z(3)
    from_far(2)
    wait_dy(order[2])
    from_sibling(2)
    wait_dy(order[3])
    for k in range(4):
        remote(late_block(0), late_block(0), lcsend.at[0], lcrecv.at[k], sibling).wait_recv()
    compute((2,), late=True)
    from_far(3)
    from_sibling(3)
    w_forward().wait_send()
    compute((3,), last=True)
    piece = wv.at[pl.ds(0, ROWS), pl.ds(0, TILE)]
    owned = got.at[0, 0]
    crossing, writes = [], []
    for load in loads:
        load.wait()

    def finish(t, slot):
        cols = pl.ds(pl.multiple_of(t * TILE, TILE), TILE)
        total = terms[t, 0].astype(jnp.float32) + terms[t, 1].astype(jnp.float32)
        decoded = total * up[:, cols].astype(jnp.float32) / 4.0
        new_moment = momentum_coef * mom[:, cols] + decoded
        mom[:, cols] = new_moment
        rows_out[:, cols] = (rows_in[:, cols].astype(jnp.float32) - outer_rate * (decoded + momentum_coef * new_moment)).astype(jnp.bfloat16)
        writes = [pltpu.make_async_copy(mom.at[:, cols], nm_ref.at[:, cols], out.at[slot, 0]),
                  pltpu.make_async_copy(rows_out.at[:, cols], np_ref.at[:, cols], out.at[slot, 1])]
        for write in writes:
            write.start()
        return writes

    def finish_pair(i):
        t, u = 2 * i + c, 2 * i + 1 - c
        remote(owned, owned, fsend.at[i], frecv.at[i], other_half).wait_recv()
        there = terms.at[t, 1 - zh]
        after = remote(there, there, bsend.at[i, 1], brecv.at[i, 1], sibling)
        after.start()
        crossing.append(after)
        writes.extend(finish(t, 2 * i))
        for j in range(2):
            remote(owned, owned, bsend.at[i, j], brecv.at[i, j], sibling).wait_recv()
        writes.extend(finish(u, 2 * i + 1))

    for i in range(TILES // 2):
        t = 2 * i + c
        cols = pl.ds(pl.multiple_of(t * TILE, TILE), TILE)
        for q in range(1, 4):
            remote(piece, owned, psend.at[0, 0], precv.at[i, q], sibling).wait_recv()

        @pl.when(c == 1)
        def _():
            pltpu.make_async_copy(piece, owned, plocal.at[i]).wait()

        @pl.when(c == 0)
        def _():
            remote(piece, owned, psend.at[0, 0], precv.at[i, 0], sibling).wait_recv()

        shrink = down[:, cols].astype(jnp.float32)

        def coded(g):
            total = got[i, 2 * g].astype(jnp.float32) + got[i, 2 * g + 1].astype(jnp.float32)
            return jnp.clip(inner_rate * (total * shrink), -code_limit, code_limit).astype(jnp.bfloat16).astype(jnp.float32)

        terms[t, zh] = (coded(0) + coded(1)).astype(jnp.bfloat16)
        here = terms.at[t, zh]
        over = remote(here, here, fsend.at[i], frecv.at[i], other_half)
        beside = remote(here, here, bsend.at[i, 0], brecv.at[i, 0], sibling)
        over.start()
        beside.start()
        crossing += [over, beside]
        if i >= LAG:
            finish_pair(i - LAG)
    for i in range(TILES // 2 - LAG, TILES // 2):
        finish_pair(i)
    @pl.when(owner)
    def _():
        give.wait_send()

    @pl.when(jnp.logical_not(owner))
    def _():
        for s in across:
            s.wait_send()

    for k in range(4):
        for j in range(4):
            remote(own, own, csend.at[k, j], crecv.at[k, j], sibling).wait_send()
        for j, n in ((0, SOON), (1, SOON), (2, cut), (3, SOON - cut)):
            src = place(y, z, c, 0, n)
            remote(src, src, ysend.at[k, j], yrecv.at[k, j], sibling).wait_send()

    for j in range(4):
        late_y(j).wait_send()
        remote(late_block(0), late_block(0), lcsend.at[j], lcrecv.at[0], sibling).wait_send()

    @pl.when(z < 3)
    def _():
        remote(own, own, zsend.at[0], zrecv.at[z], at_z(z + 1)).wait_send()
        late_z(0, z, at_z(z + 1)).wait_send()

    @pl.when(z > 0)
    def _():
        remote(own, own, zsend.at[1], zrecv.at[z], at_z(z - 1)).wait_send()
        late_z(1, z, at_z(z - 1)).wait_send()

    @pl.when(inner)
    def _():
        for n in range(1, 4):
            remote(own, own, zsend.at[1 + n], zrecv.at[0], sibling).wait_send()
            late_z(1 + n, order[n], sibling).wait_send()

    for s in near:
        s.wait_send()
    for n in range(4):
        for src, slot_to, to, k, mine in dy_parts(order[n]):
            @pl.when(jnp.logical_not(mine))
            def _():
                remote(src, dv.at[0, 0], dsend.at[k, order[n]], drecv.at[0, 0], sibling).wait_send()

    for s in crossing:
        s.wait_send()
    for t in range(TILES):
        for k, d, src, to, mine in partial_parts(t):
            @pl.when(jnp.logical_not(mine))
            def _():
                remote(src, owned, psend.at[k, t], precv.at[0, 0], sibling).wait_send()
    for write in writes:
        write.wait()


DMA = pltpu.SemaphoreType.DMA


def per_device(features, cotangent, up_rows, moment, exponents):
    bf16 = jnp.bfloat16
    f32 = jnp.float32
    return pl.pallas_call(
        work_kernel,
        out_shape=[jax.ShapeDtypeStruct((ROWS, D), bf16), jax.ShapeDtypeStruct((ROWS, D), f32)],
        in_specs=[ANY] * 4 + [pl.BlockSpec(memory_space=pltpu.VMEM)], out_specs=[ANY] * 2,
        scratch_shapes=[
            pltpu.VMEM((2, 4, 4, SEED, HALF), bf16), pltpu.VMEM((2, TOK, HALF), bf16), pltpu.VMEM((2 * ROWS, D), bf16),
            pltpu.VMEM((2, 4, 4, SEED, ROWS), bf16), pltpu.VMEM((2 * ROWS, D), f32),
            pltpu.VMEM((2, 8 * SOON, ROWS), f32), pltpu.VMEM((2 * ROWS, 8 * SOON), bf16),
            pltpu.VMEM((TILES // 2, 4, ROWS, TILE), bf16), pltpu.VMEM((TILES, 2, ROWS, TILE), bf16),
            pltpu.VMEM((ROWS, D), f32), pltpu.VMEM((ROWS, D), bf16), pltpu.VMEM((ROWS, D), bf16),
            pltpu.VMEM((ROWS, D), bf16), pltpu.VMEM((ROWS, D), bf16),
            pltpu.VMEM((ROWS, TOKENS), bf16), pltpu.VMEM((TOKENS, ROWS), f32), pltpu.VMEM((2, 4, 4, SEED, ROWS), bf16),
            DMA((2,)), DMA((2,)), DMA((5,)), DMA((4,)), DMA((4, 4)), DMA((4, 4)), DMA((4, 4)), DMA((4, 4)),
            DMA((4,)), DMA((4,)), DMA((5,)), DMA((4,)), DMA((4,)), DMA((4,)),
            DMA((3,)), DMA((2, 2)), DMA((2, 4)), DMA((2, 4)), DMA((4,)), DMA((7,)),
            DMA((2, TILES)), DMA((TILES // 2, 4)), DMA((TILES // 2,)), DMA((TILES // 2,)), DMA((TILES // 2,)),
            DMA((TILES // 2, 2)), DMA((TILES // 2, 2)), DMA((TILES, 2))],
        compiler_params=pltpu.CompilerParams(collective_id=0, has_side_effects=True, vmem_limit_bytes=60 * 2**20), name="work",
    )(features, up_rows, cotangent.T, moment, exponents.T)


def solution(mesh):
    return jax.shard_map(
        per_device,
        mesh=mesh,
        in_specs=(P(("rep", "fsdp"), None), P("rep", "fsdp"), P("fsdp", None), P("fsdp", None), P("fsdp", None)),
        out_specs=(P("fsdp", None), P("fsdp", None)),
        check_vma=False,
    )
```

```python
import functools

import jax
import jax.numpy as jnp
from jax import lax
from jax.experimental import pallas as pl
from jax.experimental.pallas import tpu as pltpu
from jax.sharding import PartitionSpec as P

inner_rate = 0.02
outer_rate = 0.7
momentum_coef = 0.9
code_limit = 448.0

D = 4096
HALF = D // 2
TOK = 56
SEED = 2 * TOK
LATE = 16
SOON = SEED - LATE
EARLY = 48
WIDE = 1024
TOKENS = 3584
ROWS = 224
HROWS = ROWS // 2
TILE = 256
TILES = D // TILE
LAG = 2
MESH = pl.DeviceIdType.MESH
ANY = pl.BlockSpec(memory_space=pl.ANY)


def where_am_i():
    rep, at = lax.axis_index("rep"), lax.axis_index("fsdp")
    return rep // 2, rep % 2, at // 16, (at // 4) % 4, at % 4


def device(zh, c, y, x, z):
    return (zh * 2 + c, (y * 4 + x) * 4 + z)


def barrier(peers):
    sem = pltpu.get_barrier_semaphore()
    for peer in peers:
        pl.semaphore_signal(sem, inc=1, device_id=peer, device_id_type=MESH)
    pl.semaphore_wait(sem, len(peers))


def remote(src, dst, send_sem, recv_sem, peer):
    return pltpu.make_async_remote_copy(src, dst, send_sem, recv_sem, device_id=peer, device_id_type=MESH)


def slope(p):
    s = jax.nn.sigmoid(p)
    return s * (1.0 + p * (1.0 - s))


def work_kernel(f_ref, w_ref, d_ref, m_ref, e_ref, np_ref, nm_ref,
                xs, seed, wv, dv, acc, pre, ht, got, terms, mom, rows_in, rows_out, up, down, dt, turned, dn,
                seed_send, seed_recv, zsend, zrecv, ysend, yrecv, csend, crecv, lysend, lyrecv, lzsend, lzrecv, lcsend, lcrecv, wsend, wrecv, dsend, drecv, dlocal, local,
                psend, precv, plocal, fsend, frecv, bsend, brecv, out):
    zh, c, y, x, z = where_am_i()
    role = 1 - c

    def at_y(k):
        return device(zh, c, (y + k) % 4, x, z)

    sibling = device(zh, 1 - c, y, x, z)
    peers = [sibling, at_y(1), at_y(3)]
    peers += [device(zh, c, y, x, (z + k) % 4) for k in range(1, 4)]
    peers += [device(zh, k, y, (x + q) % 4, z) for q in range(1, 4) for k in range(2)]
    keep_w = pltpu.make_async_copy(w_ref, wv.at[pl.ds(0, ROWS)], local.at[1])

    load_d = pltpu.make_async_copy(d_ref, dt, local.at[0])
    load_d.start()

    @pl.when(role == 0)
    def _():
        keep_w.start()

    other_half = device(1 - zh, c, y, x, z)
    barrier(peers + [other_half])
    loads = [pltpu.make_async_copy(m_ref, mom, local.at[4]), pltpu.make_async_copy(w_ref, rows_in, local.at[5])]
    for load in loads:
        load.start()

    mirror = 3 - x
    owner = c == x // 2
    whole = f_ref.at[:, pl.ds(0, HALF)]

    def half(k):
        return f_ref.at[:, pl.ds(pl.multiple_of(k * HALF, HALF), HALF)]

    keep = pltpu.make_async_copy(half(c), seed.at[0], local.at[6])
    give = remote(half(1 - c), seed.at[0], seed_send.at[0], seed_recv.at[0], sibling)
    across = [remote(half(k), seed.at[1], seed_send.at[k], seed_recv.at[1], device(zh, k, y, mirror, z)) for k in range(2)]

    @pl.when(owner)
    def _():
        keep.start()
        give.start()

    @pl.when(jnp.logical_not(owner))
    def _():
        for s in across:
            s.start()

    near = []
    for k in range(2):
        src = w_ref.at[pl.ds(pl.multiple_of(c * HROWS, 16), HROWS)]
        dst = wv.at[pl.ds(pl.multiple_of((1 - k) * ROWS + c * HROWS, 16), HROWS)]
        near.append(remote(src, dst, wsend.at[k], wrecv.at[1 - k, c], device(zh, 1 - k, y, (x + 3 + 2 * k) % 4, z)))

    for k in range(2):
        @pl.when(x % 2 != k)
        def _():
            near[k].start()

    def place(yy, zz, core, lo=0, n=SOON):
        return xs.at[core, zz, yy, pl.ds(lo, n)]

    own = place(y, z, c)

    inner = (z == 1) | (z == 2)
    order = [z, z + 1 - 2 * (z % 2), jnp.where(z < 2, 2, 1), jnp.where(z < 2, 3, 0)]

    def at_z(zz):
        return device(zh, c, y, x, zz)

    def send_own(lo, n):
        src = place(y, z, c, lo, n)

        @pl.when(z < 3)
        def _():
            remote(src, src, zsend.at[0], zrecv.at[z], at_z(z + 1)).start()

        @pl.when(z > 0)
        def _():
            remote(src, src, zsend.at[1], zrecv.at[z], at_z(z - 1)).start()

        pass_on(0, lo, n)

    def pass_on(n, lo=0, rows=SOON):
        zz = order[n]
        src = place(y, zz, c, lo, rows)
        remote(src, src, ysend.at[n, 0], yrecv.at[zz, 0], at_y(1)).start()
        remote(src, src, ysend.at[n, 1], yrecv.at[zz, 1], at_y(3)).start()
        remote(src, src, csend.at[n, 0], crecv.at[zz, 0], sibling).start()

    @pl.when(owner)
    def _():
        keep.wait()

    @pl.when(jnp.logical_not(owner))
    def _():
        remote(whole, seed.at[0], seed_send.at[0], seed_recv.at[0], sibling).wait_recv()

    xs[c, z, y, pl.ds(0, EARLY)] = seed[0, pl.ds(0, EARLY)]
    send_own(0, EARLY)

    load_d.wait()
    for b in range(TOKENS // 256):
        turned[pl.ds(b * 256, 256), :] = dt[:, pl.ds(b * 256, 256)].astype(jnp.float32).T
    remote(whole, seed.at[1], seed_send.at[0], seed_recv.at[1], sibling).wait_recv()
    joined = jnp.concatenate([seed[0].astype(jnp.float32), seed[1].astype(jnp.float32)], axis=0)
    xs[c, z, y, pl.ds(EARLY, SEED - EARLY)] = joined[EARLY:].astype(jnp.bfloat16)
    send_own(EARLY, SOON - EARLY)

    def from_z(n):
        src = place(y, order[n], c)
        remote(src, src, zsend.at[1 + n], zrecv.at[order[n]], sibling).wait_recv()

        @pl.when(inner)
        def _():
            to = 3 - z if n == 1 else jnp.where(z == 1, 0, 3)
            remote(src, src, zsend.at[1 + n], zrecv.at[order[n]], at_z(to)).start()

        pass_on(n)

    def late(yy, k=None):
        if k is None:
            return xs.at[c, z, yy, pl.ds(SOON, LATE)]
        return xs.at[c, z, yy, pl.ds(SOON, LATE), pl.ds(k * (HALF // 2), HALF // 2)]

    def late_y(j):
        src = [late(y), late(y), late((y + 3) % 4, 0), late((y + 1) % 4, 1)][j]
        return remote(src, src, lysend.at[j], lyrecv.at[j], at_y(1 if j % 2 == 0 else 3))

    def late_block(zz):
        return xs.at[c, zz, :, pl.ds(SOON, LATE)]

    def late_z(k, zz, to):
        return remote(late_block(zz), late_block(zz), lzsend.at[k], lzrecv.at[zz], to)

    def late_share(n):
        src = late_block(order[n])
        remote(src, src, lcsend.at[n], lcrecv.at[order[n]], sibling).start()

    def late_from_z(n):
        late_z(1 + n, order[n], sibling).wait_recv()

        @pl.when(inner)
        def _():
            late_z(1 + n, order[n], at_z(3 - z if n == 1 else jnp.where(z == 1, 0, 3))).start()

        late_share(n)

    late_y(0).start()
    late_y(1).start()

    def w_forward():
        row = (1 - role) * HROWS
        src = wv.at[pl.ds(pl.multiple_of((1 - role) * ROWS + row, 16), HROWS)]
        dst = wv.at[pl.ds(pl.multiple_of(ROWS + row, 16), HROWS)]
        return remote(src, dst, wsend.at[2], wrecv.at[1, 1 - role], device(zh, 0, y, (x + 3 + 2 * role) % 4, z))

    def forward_w():
        remote(w_ref.at[pl.ds(0, HROWS)], wv.at[pl.ds(0, HROWS)], wsend.at[2], wrecv.at[1 - role, 1 - role], sibling).wait_recv()
        w_forward().start()

    def wait_w():
        def arrived(k, j):
            remote(w_ref.at[pl.ds(0, HROWS)], wv.at[pl.ds(0, HROWS)], wsend.at[2], wrecv.at[k, j], sibling).wait_recv()

        arrived(1 - role, role)

        @pl.when(role == 0)
        def _():
            keep_w.wait()

        @pl.when(role == 1)
        def _():
            arrived(1, 0)
            arrived(1, 1)

    def make_dy(zz):
        for h, pair in enumerate(((0, 3), (1, 2))):
            for yy in range(4):
                pair_of = [jnp.where(c == 0, pair[0], pair[1]), jnp.where(c == 0, pair[1], pair[0])]
                both = [turned[pl.ds(pl.multiple_of(((yy * 4 + at) * 4 + zz) * TOK, 8), TOK), :] for at in pair_of]
                dn[h, zz, yy] = jnp.concatenate(both, axis=0).astype(jnp.bfloat16)

    def dy_parts(zz):
        for k in range(2):
            to = 2 * c + k
            d = (x - to + 4) % 4
            h = jnp.where((to == 0) | (to == 3), 0, 1)
            yield dn.at[h, zz], (d + d // 2) % 2, device(zh, 1 - d // 2, y, to, z), k, (d == 0) & (c == 1)

    def send_dy(zz):
        for src, slot_to, to, k, mine in dy_parts(zz):
            @pl.when(mine)
            def _():
                pltpu.make_async_copy(src, dv.at[0, zz], dlocal.at[zz]).start()

            @pl.when(jnp.logical_not(mine))
            def _():
                remote(src, dv.at[slot_to, zz], dsend.at[k, zz], drecv.at[slot_to, zz], to).start()

    def wait_dy(zz):
        here = (c == 1) & (x // 2 == 1)

        @pl.when(here)
        def _():
            pltpu.make_async_copy(dn.at[0, zz], dv.at[0, zz], dlocal.at[zz]).wait()

        @pl.when(jnp.logical_not(here))
        def _():
            remote(dn.at[0, zz], dv.at[0, zz], dsend.at[0, zz], drecv.at[0, zz], sibling).wait_recv()

        remote(dn.at[0, zz], dv.at[1, zz], dsend.at[0, zz], drecv.at[1, zz], sibling).wait_recv()

    for k in range(2):
        @pl.when(x % 2 == k)
        def _():
            near[k].start()

    make_dy(order[0])
    for j in range(2):
        late_y(j).wait_recv()
        late_y(2 + j).start()

    cut = SOON // 2

    def forward(n):
        zz = order[n]
        above, below = (y + 3) % 4, (y + 1) % 4
        remote(own, place(above, zz, c), ysend.at[n, 0], yrecv.at[zz, 0], at_y(1)).wait_recv()
        src = place(above, zz, c, 0, cut)
        remote(src, src, ysend.at[n, 2], yrecv.at[zz, 2], at_y(1)).start()
        src = place(above, zz, c)
        remote(src, src, csend.at[n, 1], crecv.at[zz, 1], sibling).start()
        remote(own, place(below, zz, c), ysend.at[n, 1], yrecv.at[zz, 1], at_y(3)).wait_recv()
        src = place(below, zz, c, cut, SOON - cut)
        remote(src, src, ysend.at[n, 3], yrecv.at[zz, 3], at_y(3)).start()
        src = place(below, zz, c)
        remote(src, src, csend.at[n, 2], crecv.at[zz, 2], sibling).start()

    def from_far(n):
        zz, far = order[n], (y + 2) % 4
        src = place(far, zz, c, 0, cut)
        remote(src, src, ysend.at[n, 2], yrecv.at[zz, 2], at_y(1)).wait_recv()
        src = place(far, zz, c, cut, SOON - cut)
        remote(src, src, ysend.at[n, 3], yrecv.at[zz, 3], at_y(3)).wait_recv()
        src = place(far, zz, c)
        remote(src, src, csend.at[n, 3], crecv.at[zz, 3], sibling).start()

    def from_sibling(n):
        for j in range(4):
            remote(own, own, csend.at[n, j], crecv.at[order[n], j], sibling).wait_recv()

    def partial_parts(t):
        for k in range(2):
            d = k + role * (3 - 2 * k)
            src = wv.at[pl.ds(k * ROWS, ROWS), pl.ds(pl.multiple_of(t * TILE, TILE), TILE)]
            to = device(zh, t % 2, y, (x + d) % 4, z)
            yield k, d, src, to, (d == 0) & (c == t % 2)

    def send_partials(t):
        for k, d, src, to, mine in partial_parts(t):
            @pl.when(mine)
            def _():
                pltpu.make_async_copy(src, got.at[t // 2, x], plocal.at[t // 2]).start()

            @pl.when(jnp.logical_not(mine))
            def _():
                remote(src, got.at[t // 2, x], psend.at[k, t], precv.at[t // 2, (4 - d) % 4], to).start()

    def compute(soon=(), late=False, first=False, last=False):
        tokens = 4 * SOON * len(soon) + 16 * LATE * late

        def x_of(h, cols):
            parts = [xs[h, order[n], :, pl.ds(0, SOON), cols] for n in soon]
            if late:
                parts.append(xs[h, :, :, pl.ds(SOON, LATE), cols])
            return jnp.concatenate([p.reshape(-1, p.shape[-1]) for p in parts], axis=0)

        def dy_of(k):
            parts = [dv[k, order[n], :, pl.ds(0, SOON), :] for n in soon]
            if late:
                parts.append(dv[k, :, :, pl.ds(SOON, LATE), :])
            return jnp.concatenate([p.reshape(-1, ROWS) for p in parts], axis=0)

        for k in range(2):
            for h in range(2):
                wt = wv[pl.ds(k * ROWS, ROWS), pl.ds(h * HALF, HALF)]
                q = lax.dot_general(x_of(h, slice(None)), wt, (((1,), (1,)), ((), ())), preferred_element_type=jnp.float32)
                if h == 0:
                    pre[k, pl.ds(0, tokens)] = q
                else:
                    pre[k, pl.ds(0, tokens)] += q
        for k in range(2):
            hid = dy_of(k).astype(jnp.float32) * slope(pre[k, pl.ds(0, tokens)])
            ht[pl.ds(k * ROWS, ROWS), pl.ds(0, tokens)] = hid.T.astype(jnp.bfloat16)
        for h in range(2):
            @pl.loop(0, HALF // WIDE)
            def _(t):
                cols = pl.ds(pl.multiple_of(t * WIDE, WIDE), WIDE)
                wide = pl.ds(pl.multiple_of(h * HALF + t * WIDE, WIDE), WIDE)
                g = jnp.dot(ht[:, pl.ds(0, tokens)], x_of(h, cols), preferred_element_type=jnp.float32)
                if not first:
                    g = g + acc[:, wide]
                if not last:
                    acc[:, wide] = g
                else:
                    wv[:, wide] = g.astype(jnp.bfloat16)
                    for j in range(WIDE // TILE):
                        send_partials((h * HALF // WIDE + t) * (WIDE // TILE) + j)

    power = e_ref[...].astype(jnp.float32).T
    bigger, smaller = jnp.exp2(power), jnp.exp2(-power)
    for b in range(D // 128):
        cols = pl.ds(b * 128, 128)
        up[:, cols] = jnp.broadcast_to(bigger[:, b:b + 1], (ROWS, 128)).astype(jnp.bfloat16)
        down[:, cols] = jnp.broadcast_to(smaller[:, b:b + 1], (ROWS, 128)).astype(jnp.bfloat16)

    for j in range(2):
        late_y(2 + j).wait_recv()

    late_share(0)
    for n in range(1, 4):
        make_dy(order[n])
    from_z(1)
    forward(0)
    from_z(2)
    forward_w()
    send_dy(order[0])
    send_dy(order[1])
    forward(1)
    from_z(3)
    @pl.when(z < 3)
    def _():
        late_z(0, z, at_z(z + 1)).start()

    @pl.when(z > 0)
    def _():
        late_z(1, z, at_z(z - 1)).start()

    from_far(0)
    forward(2)
    late_from_z(1)
    wait_w()
    wait_dy(order[0])
    send_dy(order[2])
    send_dy(order[3])
    from_sibling(0)
    late_from_z(2)
    from_far(1)
    wait_dy(order[1])
    from_sibling(1)
    compute((0, 1), first=True)
    forward(3)
    late_from_z(3)
    from_far(2)
    wait_dy(order[2])
    from_sibling(2)
    wait_dy(order[3])
    for k in range(4):
        remote(late_block(0), late_block(0), lcsend.at[0], lcrecv.at[k], sibling).wait_recv()
    compute((2,), late=True)
    from_far(3)
    from_sibling(3)
    w_forward().wait_send()
    compute((3,), last=True)
    piece = wv.at[pl.ds(0, ROWS), pl.ds(0, TILE)]
    owned = got.at[0, 0]
    crossing, writes = [], []
    for load in loads:
        load.wait()

    def finish(t, slot):
        cols = pl.ds(pl.multiple_of(t * TILE, TILE), TILE)
        total = terms[t, 0].astype(jnp.float32) + terms[t, 1].astype(jnp.float32)
        decoded = total * up[:, cols].astype(jnp.float32) / 4.0
        new_moment = momentum_coef * mom[:, cols] + decoded
        mom[:, cols] = new_moment
        rows_out[:, cols] = (rows_in[:, cols].astype(jnp.float32) - outer_rate * (decoded + momentum_coef * new_moment)).astype(jnp.bfloat16)
        writes = [pltpu.make_async_copy(mom.at[:, cols], nm_ref.at[:, cols], out.at[slot, 0]),
                  pltpu.make_async_copy(rows_out.at[:, cols], np_ref.at[:, cols], out.at[slot, 1])]
        for write in writes:
            write.start()
        return writes

    def finish_pair(i):
        t, u = 2 * i + c, 2 * i + 1 - c
        remote(owned, owned, fsend.at[i], frecv.at[i], other_half).wait_recv()
        there = terms.at[t, 1 - zh]
        after = remote(there, there, bsend.at[i, 1], brecv.at[i, 1], sibling)
        after.start()
        crossing.append(after)
        writes.extend(finish(t, 2 * i))
        for j in range(2):
            remote(owned, owned, bsend.at[i, j], brecv.at[i, j], sibling).wait_recv()
        writes.extend(finish(u, 2 * i + 1))

    for i in range(TILES // 2):
        t = 2 * i + c
        cols = pl.ds(pl.multiple_of(t * TILE, TILE), TILE)
        for q in range(1, 4):
            remote(piece, owned, psend.at[0, 0], precv.at[i, q], sibling).wait_recv()

        @pl.when(c == 1)
        def _():
            pltpu.make_async_copy(piece, owned, plocal.at[i]).wait()

        @pl.when(c == 0)
        def _():
            remote(piece, owned, psend.at[0, 0], precv.at[i, 0], sibling).wait_recv()

        shrink = down[:, cols].astype(jnp.float32)

        def coded(g):
            total = got[i, 2 * g].astype(jnp.float32) + got[i, 2 * g + 1].astype(jnp.float32)
            return jnp.clip(inner_rate * (total * shrink), -code_limit, code_limit).astype(jnp.bfloat16).astype(jnp.float32)

        terms[t, zh] = (coded(0) + coded(1)).astype(jnp.bfloat16)
        here = terms.at[t, zh]
        over = remote(here, here, fsend.at[i], frecv.at[i], other_half)
        beside = remote(here, here, bsend.at[i, 0], brecv.at[i, 0], sibling)
        over.start()
        beside.start()
        crossing += [over, beside]
        if i >= LAG:
            finish_pair(i - LAG)
    for i in range(TILES // 2 - LAG, TILES // 2):
        finish_pair(i)
    @pl.when(owner)
    def _():
        give.wait_send()

    @pl.when(jnp.logical_not(owner))
    def _():
        for s in across:
            s.wait_send()

    for k in range(4):
        for j in range(4):
            remote(own, own, csend.at[k, j], crecv.at[k, j], sibling).wait_send()
        for j, n in ((0, SOON), (1, SOON), (2, cut), (3, SOON - cut)):
            src = place(y, z, c, 0, n)
            remote(src, src, ysend.at[k, j], yrecv.at[k, j], sibling).wait_send()

    for j in range(4):
        late_y(j).wait_send()
        remote(late_block(0), late_block(0), lcsend.at[j], lcrecv.at[0], sibling).wait_send()

    @pl.when(z < 3)
    def _():
        remote(own, own, zsend.at[0], zrecv.at[z], at_z(z + 1)).wait_send()
        late_z(0, z, at_z(z + 1)).wait_send()

    @pl.when(z > 0)
    def _():
        remote(own, own, zsend.at[1], zrecv.at[z], at_z(z - 1)).wait_send()
        late_z(1, z, at_z(z - 1)).wait_send()

    @pl.when(inner)
    def _():
        for n in range(1, 4):
            remote(own, own, zsend.at[1 + n], zrecv.at[0], sibling).wait_send()
            late_z(1 + n, order[n], sibling).wait_send()

    for s in near:
        s.wait_send()
    for n in range(4):
        for src, slot_to, to, k, mine in dy_parts(order[n]):
            @pl.when(jnp.logical_not(mine))
            def _():
                remote(src, dv.at[0, 0], dsend.at[k, order[n]], drecv.at[0, 0], sibling).wait_send()

    for s in crossing:
        s.wait_send()
    for t in range(TILES):
        for k, d, src, to, mine in partial_parts(t):
            @pl.when(jnp.logical_not(mine))
            def _():
                remote(src, owned, psend.at[k, t], precv.at[0, 0], sibling).wait_send()
    for write in writes:
        write.wait()


DMA = pltpu.SemaphoreType.DMA


def per_device(features, cotangent, up_rows, moment, exponents):
    bf16 = jnp.bfloat16
    f32 = jnp.float32
    return pl.pallas_call(
        work_kernel,
        out_shape=[jax.ShapeDtypeStruct((ROWS, D), bf16), jax.ShapeDtypeStruct((ROWS, D), f32)],
        in_specs=[ANY] * 4 + [pl.BlockSpec(memory_space=pltpu.VMEM)], out_specs=[ANY] * 2,
        scratch_shapes=[
            pltpu.VMEM((2, 4, 4, SEED, HALF), bf16), pltpu.VMEM((2, TOK, HALF), bf16), pltpu.VMEM((2 * ROWS, D), bf16),
            pltpu.VMEM((2, 4, 4, SEED, ROWS), bf16), pltpu.VMEM((2 * ROWS, D), f32),
            pltpu.VMEM((2, 8 * SOON, ROWS), f32), pltpu.VMEM((2 * ROWS, 8 * SOON), bf16),
            pltpu.VMEM((TILES // 2, 4, ROWS, TILE), bf16), pltpu.VMEM((TILES, 2, ROWS, TILE), bf16),
            pltpu.VMEM((ROWS, D), f32), pltpu.VMEM((ROWS, D), bf16), pltpu.VMEM((ROWS, D), bf16),
            pltpu.VMEM((ROWS, D), bf16), pltpu.VMEM((ROWS, D), bf16),
            pltpu.VMEM((ROWS, TOKENS), bf16), pltpu.VMEM((TOKENS, ROWS), f32), pltpu.VMEM((2, 4, 4, SEED, ROWS), bf16),
            DMA((2,)), DMA((2,)), DMA((5,)), DMA((4,)), DMA((4, 4)), DMA((4, 4)), DMA((4, 4)), DMA((4, 4)),
            DMA((4,)), DMA((4,)), DMA((5,)), DMA((4,)), DMA((4,)), DMA((4,)),
            DMA((3,)), DMA((2, 2)), DMA((2, 4)), DMA((2, 4)), DMA((4,)), DMA((7,)),
            DMA((2, TILES)), DMA((TILES // 2, 4)), DMA((TILES // 2,)), DMA((TILES // 2,)), DMA((TILES // 2,)),
            DMA((TILES // 2, 2)), DMA((TILES // 2, 2)), DMA((TILES, 2))],
        compiler_params=pltpu.CompilerParams(collective_id=0, has_side_effects=True, vmem_limit_bytes=60 * 2**20), name="work",
    )(features, up_rows, cotangent.T, moment, exponents.T)


def solution(mesh):
    return jax.shard_map(
        per_device,
        mesh=mesh,
        in_specs=(P(("rep", "fsdp"), None), P("rep", "fsdp"), P("fsdp", None), P("fsdp", None), P("fsdp", None)),
        out_specs=(P("fsdp", None), P("fsdp", None)),
        check_vma=False,
    )
```
